1024 devices in a mesh: box: 64 (over y_lo, z, core), dir: 16 (over x, y_hi).
Axes of the slice: x: 8, y: 8 (y_hi: 2, y_lo: 4; y = y_hi * 4 + y_lo), z: 8, core: 2. Of those that a mesh axis runs over, the one named last changes fastest.
Arguments:
- child_out: bfloat16 [8192, 8, 512], P('box', None, 'dir'), may hold values from -6 to 6
- interp: bfloat16 [512, 2048], replicated, may hold values from -0.25 to 0.25
- shift_angle: float32 [8, 2048], replicated, may hold values from -3.140625 to 3.140625
- translators: float32 [343, 2, 2048], P(None, None, 'dir'), may hold values from -3 to 3
- nbr_index: int32 [1024, 27], replicated, may hold values from 0 to 1023, as said below
- nbr_trans: int32 [1024, 27], replicated, may hold values from 0 to 342, as said below
Outputs:
- child_in: bfloat16 [8192, 8, 512], P('box', None, 'dir')
The draws below stay inside these ranges and needn't reach their ends.
Inputs may be any that keep to these rules, and one draw needn't show every extreme that they name: Parents lie on a periodic slab indexed in Morton order: all index bits but the top two are taken in turn by the first two coordinates (lowest bit first), and the top two bits give the third coordinate, which thus runs over 4 layers. Row p holds 27 distinct offsets of largest component 2 or 3, and nbr_index[p, n] is the parent at that offset from p, coordinates taken periodically. nbr_trans[p, n] = (dx + 3) * 49 + (dy + 3) * 7 + (dz + 3) for the offset (dx, dy, dz) of nbr_index[p, n].
All inputs are finite; a program needn't handle non-finite values.
Results may differ from the reference program's by a relative error of at most 0.012.
Values may be sent and summed in bfloat16 or wider, within the bound.
A program may use at most 32 MiB of HBM per device.

```python
import jax
import jax.numpy as jnp
import numpy as np
from jax import lax

NCD = 512
NPD = 2048
CH = 8
NBR = 27
NT = 343
OCT = 8
COLS = 8
NP = 1024
NB = 8192


def partner_lists(key):
    inner = jax.random.fold_in(key, 7)
    bits = max(NP - 1, 1).bit_length()
    assign = [(bit % 2, bit // 2) for bit in range(bits - 2)] + [(2, 0), (2, 1)]
    index = jnp.arange(NP, dtype=jnp.int32)
    coords = [jnp.zeros((NP,), jnp.int32) for axis_num in range(3)]
    counts = [0, 0, 0]
    for bit in range(bits):
        which, level = assign[bit]
        coords[which] = coords[which] + index // 2 ** bit % 2 * 2 ** level
        counts[which] = counts[which] + 1
    extents = [2 ** counts[axis_num] for axis_num in range(3)]
    offsets = []
    for dx in range(-3, 4):
        for dy in range(-3, 4):
            for dz in range(-3, 4):
                if max(abs(dx), abs(dy), abs(dz)) >= 2:
                    offsets.append([dx, dy, dz, (dx + 3) * 49 + (dy + 3) * 7 + (dz + 3)])
    offsets = jnp.asarray(np.array(offsets, dtype=np.int32))
    count = offsets.shape[0]
    scores = jax.random.randint(inner, (NP, count), 0, 2 ** 20) * 512 + jnp.arange(count, dtype=jnp.int32)[None, :]
    chosen = lax.top_k(scores, NBR)[1]
    picked = offsets[chosen]
    moved = [(coords[axis_num][:, None] + picked[:, :, axis_num]) % extents[axis_num] for axis_num in range(3)]
    target = jnp.zeros((NP, NBR), jnp.int32)
    for bit in range(bits):
        which, level = assign[bit]
        target = target + moved[which] // 2 ** level % 2 * 2 ** bit
    return ((target % NP).astype(jnp.int32), picked[:, :, 3].astype(jnp.int32))


def draw_nbr_index(key, part):
    return partner_lists(key)[0]


def draw_nbr_trans(key, part):
    return partner_lists(key)[1]


def block_levels(rng, shape, shards, low, high):
    gain = 1.0
    for position, blocks in shards:
        heights = jax.random.uniform(jax.random.fold_in(jax.random.fold_in(rng, 6), position), (blocks,), jnp.float32, low / len(shards), high / len(shards))
        gain = gain * jnp.repeat(jnp.exp(heights), shape[position] // blocks).reshape((-1,) + (1,) * (len(shape) - 1 - position))
    return gain


def centred(own_key, extent, spread, bound, shards=(), kind=jnp.bfloat16):
    values = spread * jax.random.normal(own_key, extent, jnp.float32)
    if shards:
        values = values * block_levels(own_key, extent, shards, -0.22, 0.18)
    return jnp.clip(values, -bound, bound).astype(kind)


def setup_inputs(seed: int = 0) -> dict:
    arg_keys = jax.random.split(jax.random.key(seed), 7)
    child_out = centred(arg_keys[0], (NB, COLS, NCD), 1.0, 6.0, ((0, 64), (2, 16)))
    interp = centred(arg_keys[1], (NCD, NPD), NCD ** -0.5, 0.25)
    shift_angle = jnp.clip(jax.random.uniform(arg_keys[2], (OCT, NPD), jnp.float32, -3.140625, 3.140625), -3.140625, 3.140625)
    translators = centred(arg_keys[3], (NT, 2, NPD), 0.2, 3.0, ((2, 16),), jnp.float32)
    nbr_index = draw_nbr_index(jax.random.fold_in(arg_keys[6], 71), 0)
    nbr_trans = draw_nbr_trans(jax.random.fold_in(arg_keys[6], 71), 0)
    return dict(child_out=child_out, interp=interp, shift_angle=shift_angle, translators=translators, nbr_index=nbr_index, nbr_trans=nbr_trans)


def cmul(field, real_part, imag_part):
    half = field.shape[-2] // 2
    left = field[..., :half, :]
    right = field[..., half:, :]
    return jnp.concatenate([left * real_part - right * imag_part, left * imag_part + right * real_part], axis=-2)


def reference(child_out, interp, shift_angle, translators, nbr_index, nbr_trans):
    cols = child_out.shape[1]
    interp_child = jnp.dot(child_out.reshape(NB * cols, NCD), interp, preferred_element_type=jnp.float32).reshape(NB, cols, NPD)
    octants = (jnp.arange(NB, dtype=jnp.int32) % CH).astype(jnp.int32)
    cosine = jnp.cos(shift_angle)[octants][:, None, :]
    sine = jnp.sin(shift_angle)[octants][:, None, :]
    shifted = cmul(interp_child, cosine, sine)
    parent_out = shifted.reshape(NP, CH, cols, NPD).sum(axis=1).astype(jnp.bfloat16)
    parent_in = jnp.zeros((NP, cols, NPD), jnp.float32)
    for slot in range(NBR):
        source = parent_out[nbr_index[:, slot]].astype(jnp.float32)
        table = translators[nbr_trans[:, slot]]
        parent_in = parent_in + cmul(source, table[:, 0:1, :], table[:, 1:2, :])
    parent_in = parent_in.astype(jnp.bfloat16)
    down = jnp.repeat(parent_in, CH, axis=0).astype(jnp.float32)
    back = cmul(down, cosine, -sine).astype(jnp.bfloat16)
    result = jnp.dot(back.reshape(NB * cols, NPD), interp.T, preferred_element_type=jnp.float32)
    return (0.125 * result).reshape(NB, cols, NCD).astype(jnp.bfloat16)
```

```python
import jax
import jax.numpy as jnp
from jax import lax
from jax.experimental import pallas as pl
from jax.experimental.pallas import tpu as pltpu
from jax.sharding import PartitionSpec as P

MESH = pl.DeviceIdType.MESH
F32 = jnp.float32
BF16 = jnp.bfloat16

NCD = 512
NPD = 2048
NBR = 27
NT = 343
NDIR = 16
RHS = 4
LAYERS = 4
BLK = 16
LANES = 128
GROUP = LAYERS * BLK
EDGE = 48
HALO = GROUP + 8 * EDGE
HALO_PAD = 512
NT_PAD = 384
STEP = 9
TURNS = [m for m in range(9) if m != 4]


def swap_lane_blocks(tiles):
    lane = lax.broadcasted_iota(jnp.int32, tiles[0].shape, 1)
    low = (lane // 32) % 2 == 0
    mid = (lane // 64) % 2 == 0
    v0, v1, v2, v3 = tiles

    def pair(a, b, keep, width):
        first = jnp.where(keep, a, pltpu.roll(b, width, 1))
        second = jnp.where(keep, pltpu.roll(a, LANES - width, 1), b)
        return first, second

    v0, v1 = pair(v0, v1, low, 32)
    v2, v3 = pair(v2, v3, low, 32)
    v0, v2 = pair(v0, v2, mid, 64)
    v1, v3 = pair(v1, v3, mid, 64)
    return [v0, v1, v2, v3]


def kernel(
    child_hbm, interp_hbm, angle_hbm, trans_hbm, nidx_hbm, ntr_hbm, out_ref,
    child_v, interp_v, angle_v, trans_v, nidx_v, ntr_v,
    send_a, recv_a, lhs_v, cos_v, sin_v, send_p, recv_p, field_v, turned_v,
    pick_v, factor_v, table_hi, table_lo, send_q, recv_q, back_v, send_c, recv_c,
    load_sem, send_sem, recv_sem,
):
    box = lax.axis_index("box")
    me = lax.axis_index("dir")
    layer = box // 16
    zc = box % 16
    xb = zc % 2 + 2 * ((zc // 4) % 2)
    yb = (zc // 2) % 2 + 2 * (zc // 8)

    loads = [
        pltpu.make_async_copy(src, dst, load_sem.at[i])
        for i, (src, dst) in enumerate(
            [
                (child_hbm, child_v),
                (angle_hbm, angle_v),
                (nidx_hbm, nidx_v),
                (ntr_hbm, ntr_v),
                (interp_hbm, interp_v),
                (trans_hbm, trans_v),
            ]
        )
    ]
    for load in loads:
        load.start()

    def plane(t):
        return (layer + t // NDIR) % LAYERS, (me + t) % NDIR

    def neighbour(m):
        dx, dy = m % 3 - 1, m // 3 - 1
        tx, ty = (xb - dx + 4) % 4, (yb - dy + 4) % 4
        return layer * 16 + tx % 2 + 2 * (ty % 2) + 4 * (tx // 2) + 8 * (ty // 2)

    barrier = pltpu.get_barrier_semaphore()

    def greet(t, carry):
        to_layer, to_dir = plane(t)
        pl.semaphore_signal(
            barrier, inc=1, device_id=(to_layer * 16 + zc, to_dir), device_id_type=MESH
        )
        return carry

    lax.fori_loop(1, LAYERS * NDIR, greet, 0)
    for m in TURNS:
        pl.semaphore_signal(barrier, inc=1, device_id=(neighbour(m), me), device_id_type=MESH)

    loads[0].wait()
    halves = []
    for h in range(2):
        block = child_v[h * LANES : (h + 1) * LANES, :].astype(F32)
        halves.append(block.T.reshape(NDIR, 8, LANES))
    send_a[...] = jnp.concatenate(halves, axis=1).astype(BF16)

    pl.semaphore_wait(barrier, LAYERS * NDIR - 1 + len(TURNS))

    def send_child(t, carry):
        to = (me + t) % NDIR
        pltpu.make_async_remote_copy(
            src_ref=send_a.at[to], dst_ref=recv_a.at[me],
            send_sem=send_sem.at[0], recv_sem=recv_sem.at[0],
            device_id=(box, to), device_id_type=MESH,
        ).start()
        return carry

    lax.fori_loop(1, NDIR, send_child, 0)
    recv_a[me] = send_a[me]

    loads[1].wait()
    cos_v[...] = jnp.cos(angle_v[...])
    sin_v[...] = jnp.sin(angle_v[...])

    loads[2].wait()
    loads[3].wait()
    lane = lax.broadcasted_iota(jnp.int32, (32, LANES), 1)

    def mine(ref):
        parts = jnp.zeros((32, LANES), jnp.int32)
        for q in range(LAYERS):
            at = pl.multiple_of(q * 256 + (zc // 8) * LANES, LANES)
            cols = jnp.concatenate(
                [ref[:, pl.ds(at, LANES)], jnp.zeros((32 - NBR, LANES), jnp.int32)], axis=0
            )
            cols = pltpu.roll(cols, (q * BLK - (zc % 8) * BLK + LANES) % LANES, 1)
            parts = jnp.where(lane // BLK == q, cols, parts)
        return parts

    source = mine(nidx_v)
    sx = source % 2 + 2 * ((source // 4) % 2) + 4 * ((source // 16) % 2) + 8 * ((source // 64) % 2)
    sy = (source // 2) % 2 + 2 * ((source // 8) % 2) + 4 * ((source // 32) % 2) + 8 * ((source // 128) % 2)
    sl = source // 256
    u = (sx - 4 * xb + 20) % 16
    v = (sy - 4 * yb + 20) % 16
    bx, x, by, y = u // 4, u % 4, v // 4, v % 4
    turn = by * 3 + bx
    base = GROUP + EDGE * (turn - (turn > 4).astype(jnp.int32))
    by_y = base + 16 * (y - (by == 0).astype(jnp.int32)) + 4 * x + sl
    by_x = base + 16 * (x - (bx == 0).astype(jnp.int32)) + 4 * y + sl
    row = jnp.where(by != 1, by_y, jnp.where(bx != 1, by_x, 16 * y + 4 * x + sl))
    source_rows = row.astype(F32).T[0:GROUP, :]
    factor_rows = mine(ntr_v).astype(F32).T[0:GROUP, :]

    slot_no = lax.broadcasted_iota(jnp.int32, (GROUP, HALO_PAD), 1).astype(F32)
    for n in range(NBR):
        pick_v[n * GROUP : (n + 1) * GROUP, :] = jnp.where(
            source_rows[:, n : n + 1] == slot_no, 1.0, 0.0
        ).astype(BF16)

    loads[4].wait()
    pltpu.make_async_copy(
        recv_a.at[pl.ds(0, NDIR - 1)], recv_a.at[pl.ds(0, NDIR - 1)], recv_sem.at[0]
    ).wait()
    for g in range(4):
        tiles = swap_lane_blocks([recv_a[4 * g + i].astype(F32) for i in range(4)])
        for c in range(4):
            lhs_v[c * 16 : (c + 1) * 16, g * LANES : (g + 1) * LANES] = tiles[c].astype(BF16)
    for d2 in range(NDIR // 2):
        prod = jnp.dot(
            lhs_v[...], interp_v[:, d2 * 256 : (d2 + 1) * 256], preferred_element_type=F32
        )
        for i in range(2):
            d = d2 * 2 + i
            cosine = cos_v[:, d * LANES : (d + 1) * LANES]
            sine = sin_v[:, d * LANES : (d + 1) * LANES]
            for c in range(RHS):
                re = prod[c * 16 : c * 16 + 8, i * LANES : (i + 1) * LANES]
                im = prod[c * 16 + 8 : c * 16 + 16, i * LANES : (i + 1) * LANES]
                out_re = jnp.sum(re * cosine - im * sine, axis=0, keepdims=True)
                out_im = jnp.sum(re * sine + im * cosine, axis=0, keepdims=True)
                send_p[d * RHS + c, 0:1, :] = out_re.astype(BF16).astype(F32)
                send_p[d * RHS + c, 1:2, :] = out_im.astype(BF16).astype(F32)

    my_row = 16 * ((me // 2) % 2 + 2 * (me // 8)) + 4 * (me % 2 + 2 * ((me // 4) % 2)) + layer

    def send_parent(t, carry):
        to_layer, to_dir = plane(t)
        pltpu.make_async_remote_copy(
            src_ref=send_p.at[to_dir * RHS + to_layer], dst_ref=recv_p.at[my_row],
            send_sem=send_sem.at[1], recv_sem=recv_sem.at[1],
            device_id=(to_layer * 16 + zc, to_dir), device_id_type=MESH,
        ).start()
        return carry

    lax.fori_loop(1, LAYERS * NDIR, send_parent, 0)
    recv_p[my_row] = send_p[me * RHS + layer]

    loads[5].wait()
    for h in range(2):
        values = trans_v[:, h, :]
        hi = values.astype(BF16)
        lo = (values - hi.astype(F32)).astype(BF16)
        pad = jnp.zeros((NT_PAD - NT, LANES), BF16)
        table_hi[:, h * LANES : (h + 1) * LANES] = jnp.concatenate([hi, pad], axis=0)
        table_lo[:, h * LANES : (h + 1) * LANES] = jnp.concatenate([lo, pad], axis=0)
    field_v[HALO:HALO_PAD, :] = jnp.zeros((HALO_PAD - HALO, 2 * LANES), BF16)

    pltpu.make_async_copy(
        recv_p.at[pl.ds(0, GROUP - 1)], recv_p.at[pl.ds(0, GROUP - 1)], recv_sem.at[1]
    ).wait()
    for h in range(2):
        cols = slice(h * LANES, (h + 1) * LANES)
        field_v[0:GROUP, cols] = recv_p[:, h, :].astype(BF16)
        turned_v[:, cols] = jnp.concatenate(
            [recv_p[16 * gy + 4 * gx : 16 * gy + 4 * gx + 4, h, :] for gx in range(4) for gy in range(4)],
            axis=0,
        ).astype(BF16)

    for k, m in enumerate(TURNS):
        dx, dy = m % 3 - 1, m // 3 - 1
        first = 16 if (dy if dy else dx) < 0 else 0
        pltpu.make_async_remote_copy(
            src_ref=(field_v if dy else turned_v).at[pl.ds(first, EDGE)],
            dst_ref=field_v.at[pl.ds(GROUP + EDGE * k, EDGE)],
            send_sem=send_sem.at[2], recv_sem=recv_sem.at[2],
            device_id=(neighbour(m), me), device_id_type=MESH,
        ).start()

    factor_no = lax.broadcasted_iota(jnp.int32, (GROUP, NT_PAD), 1).astype(F32)
    for s in range(0, NBR, STEP):
        chosen = jnp.concatenate(
            [
                jnp.where(factor_rows[:, n : n + 1] == factor_no, 1.0, 0.0).astype(BF16)
                for n in range(s, s + STEP)
            ],
            axis=0,
        )
        factor_v[s * GROUP : (s + STEP) * GROUP, :] = jnp.dot(
            chosen, table_hi[...], preferred_element_type=F32
        ) + jnp.dot(chosen, table_lo[...], preferred_element_type=F32)

    arrived = field_v.at[pl.ds(GROUP, 8 * EDGE)]
    pltpu.make_async_copy(arrived, arrived, recv_sem.at[2]).wait()
    sum_re = jnp.zeros((GROUP, LANES), F32)
    sum_im = jnp.zeros((GROUP, LANES), F32)
    for s in range(0, NBR, STEP):
        picked = jnp.dot(
            pick_v[s * GROUP : (s + STEP) * GROUP, :], field_v[...], preferred_element_type=F32
        )
        for n in range(STEP):
            re = picked[n * GROUP : (n + 1) * GROUP, 0:LANES]
            im = picked[n * GROUP : (n + 1) * GROUP, LANES : 2 * LANES]
            at = (s + n) * GROUP
            t_re = factor_v[at : at + GROUP, 0:LANES]
            t_im = factor_v[at : at + GROUP, LANES : 2 * LANES]
            sum_re = sum_re + (re * t_re - im * t_im)
            sum_im = sum_im + (re * t_im + im * t_re)
    send_q[:, 0, :] = sum_re.astype(BF16).astype(F32)
    send_q[:, 1, :] = sum_im.astype(BF16).astype(F32)

    def send_sum(t, carry):
        to_layer, to_dir = plane(t)
        pltpu.make_async_remote_copy(
            src_ref=send_q.at[to_layer * BLK + to_dir], dst_ref=recv_q.at[me * RHS + layer],
            send_sem=send_sem.at[3], recv_sem=recv_sem.at[3],
            device_id=(to_layer * 16 + zc, to_dir), device_id_type=MESH,
        ).start()
        return carry

    lax.fori_loop(1, LAYERS * NDIR, send_sum, 0)
    recv_q[me * RHS + layer] = send_q[layer * BLK + me]

    pltpu.make_async_copy(
        recv_q.at[pl.ds(0, GROUP - 1)], recv_q.at[pl.ds(0, GROUP - 1)], recv_sem.at[3]
    ).wait()
    for d in range(NDIR):
        cosine = cos_v[:, d * LANES : (d + 1) * LANES]
        sine = sin_v[:, d * LANES : (d + 1) * LANES]
        for c in range(RHS):
            re = recv_q[d * RHS + c, 0:1, :]
            im = recv_q[d * RHS + c, 1:2, :]
            back_v[c * 16 : (c + 1) * 16, d * LANES : (d + 1) * LANES] = jnp.concatenate(
                [re * cosine + im * sine, im * cosine - re * sine], axis=0
            ).astype(BF16)
    prod = 0.125 * lax.dot_general(
        back_v[...], interp_v[...], (((1,), (1,)), ((), ())), preferred_element_type=F32
    )
    for g in range(4):
        tiles = swap_lane_blocks(
            [prod[c * 16 : (c + 1) * 16, g * LANES : (g + 1) * LANES] for c in range(4)]
        )
        for i in range(4):
            send_c[4 * g + i] = tiles[i].astype(BF16)

    def send_result(t, carry):
        to = (me + t) % NDIR
        pltpu.make_async_remote_copy(
            src_ref=send_c.at[to], dst_ref=recv_c.at[me],
            send_sem=send_sem.at[4], recv_sem=recv_sem.at[4],
            device_id=(box, to), device_id_type=MESH,
        ).start()
        return carry

    lax.fori_loop(1, NDIR, send_result, 0)
    recv_c[me] = send_c[me]
    pltpu.make_async_copy(
        recv_c.at[pl.ds(0, NDIR - 1)], recv_c.at[pl.ds(0, NDIR - 1)], recv_sem.at[4]
    ).wait()
    result = recv_c[...].astype(F32)
    for h in range(2):
        block = result[:, h * 8 : (h + 1) * 8, :].reshape(LANES, LANES)
        out_ref[h * LANES : (h + 1) * LANES, :] = block.T.astype(BF16)

    sent = [
        send_a.at[pl.ds(0, NDIR - 1)],
        send_p.at[pl.ds(0, GROUP - 1)],
        field_v.at[pl.ds(0, 8 * EDGE)],
        send_q.at[pl.ds(0, GROUP - 1)],
        send_c.at[pl.ds(0, NDIR - 1)],
    ]
    for i, ref in enumerate(sent):
        pltpu.make_async_copy(ref, ref, send_sem.at[i]).wait()


def per_device(child_out, interp, shift_angle, translators, nbr_index, nbr_trans):
    count, cols, width = child_out.shape
    children = child_out.transpose(1, 2, 0).reshape(cols * width, count)
    out = pl.pallas_call(
        kernel,
        out_shape=jax.ShapeDtypeStruct((cols * width, count), BF16),
        in_specs=[pl.BlockSpec(memory_space=pl.ANY)] * 6,
        out_specs=pl.BlockSpec(memory_space=pltpu.VMEM),
        scratch_shapes=[
            pltpu.VMEM((cols * width, count), BF16),
            pltpu.VMEM((NCD, NPD), BF16),
            pltpu.VMEM((8, NPD), F32),
            pltpu.VMEM((NT, 2, LANES), F32),
            pltpu.VMEM((NBR, 1024), jnp.int32),
            pltpu.VMEM((NBR, 1024), jnp.int32),
            pltpu.VMEM((NDIR, 16, LANES), BF16),
            pltpu.VMEM((NDIR, 16, LANES), BF16),
            pltpu.VMEM((64, NCD), BF16),
            pltpu.VMEM((8, NPD), F32),
            pltpu.VMEM((8, NPD), F32),
            pltpu.VMEM((GROUP, 2, LANES), F32),
            pltpu.VMEM((GROUP, 2, LANES), F32),
            pltpu.VMEM((HALO_PAD, 2 * LANES), BF16),
            pltpu.VMEM((GROUP, 2 * LANES), BF16),
            pltpu.VMEM((NBR * GROUP, HALO_PAD), BF16),
            pltpu.VMEM((NBR * GROUP, 2 * LANES), F32),
            pltpu.VMEM((NT_PAD, 2 * LANES), BF16),
            pltpu.VMEM((NT_PAD, 2 * LANES), BF16),
            pltpu.VMEM((GROUP, 2, LANES), F32),
            pltpu.VMEM((GROUP, 2, LANES), F32),
            pltpu.VMEM((64, NPD), BF16),
            pltpu.VMEM((NDIR, 16, LANES), BF16),
            pltpu.VMEM((NDIR, 16, LANES), BF16),
            pltpu.SemaphoreType.DMA((6,)),
            pltpu.SemaphoreType.DMA((5,)),
            pltpu.SemaphoreType.DMA((5,)),
        ],
        compiler_params=pltpu.CompilerParams(
            collective_id=0, has_side_effects=True, vmem_limit_bytes=40 * 1024 * 1024
        ),
    )(children, interp, shift_angle, translators, nbr_index.T, nbr_trans.T)
    return out.reshape(cols, width, count).transpose(2, 0, 1)


def solution(mesh):
    return jax.shard_map(
        per_device,
        mesh=mesh,
        in_specs=(P("box", None, "dir"), P(), P(), P(None, None, "dir"), P(), P()),
        out_specs=P("box", None, "dir"),
        check_vma=False,
    )
```

```python
import jax
import jax.numpy as jnp
from jax import lax
from jax.experimental import pallas as pl
from jax.experimental.pallas import tpu as pltpu
from jax.sharding import PartitionSpec as P

MESH = pl.DeviceIdType.MESH
F32 = jnp.float32
BF16 = jnp.bfloat16

NCD = 512
NPD = 2048
NBR = 27
NT = 343
NX = 8
NDIR = 16
RHS = 4
LAYERS = 4
BLK = 16
LANES = 128
PLANE = 64
GROUP = LAYERS * BLK
EDGE = 48
HALO = GROUP + 8 * EDGE
HALO_PAD = 512
NT_PAD = 384
STEP = 9
TURNS = [m for m in range(9) if m != 4]


def swap_lane_blocks(tiles):
    lane = lax.broadcasted_iota(jnp.int32, tiles[0].shape, 1)
    low = (lane // 32) % 2 == 0
    mid = (lane // 64) % 2 == 0
    v0, v1, v2, v3 = tiles

    def pair(a, b, keep, width):
        first = jnp.where(keep, a, pltpu.roll(b, width, 1))
        second = jnp.where(keep, pltpu.roll(a, LANES - width, 1), b)
        return first, second

    v0, v1 = pair(v0, v1, low, 32)
    v2, v3 = pair(v2, v3, low, 32)
    v0, v2 = pair(v0, v2, mid, 64)
    v1, v3 = pair(v1, v3, mid, 64)
    return [v0, v1, v2, v3]


def far_first(s):
    return 4 + (1 - 2 * (s % 2)) * ((s + 1) // 2)


def swap_parts(field, sign):
    part = (lax.broadcasted_iota(jnp.int32, field.shape, 0) // 2) % 2
    return jnp.where(part == 0, sign * pltpu.roll(field, 6, 0), -sign * pltpu.roll(field, 2, 0))


def kernel(
    child_hbm, interp_hbm, angle_hbm, trans_hbm, nidx_hbm, ntr_hbm, out_ref,
    child_v, interp_v, angle_v, trans_v, nidx_v, ntr_v,
    send_a, recv_a, lhs_v, cos_v, sin_v, send_p, recv_p, sum_v, field_v, turned_v, rows_v,
    pick_v, factor_v, table_hi, table_lo, send_q, recv_q, back_v, send_c, recv_c,
    load_sem, send_sem, recv_sem,
):
    box = lax.axis_index("box")
    me = lax.axis_index("dir")
    layer = box // 16
    zc = box % 16
    xb = zc % 2 + 2 * ((zc // 4) % 2)
    yb = (zc // 2) % 2 + 2 * (zc // 8)
    mx = me // 2
    half = me % 2
    my = half * 4 + layer

    def device(x, y):
        return ((y % 4) * 16 + zc, x * 2 + y // 4)

    def neighbour(m):
        dx, dy = m % 3 - 1, m // 3 - 1
        tx, ty = (xb - dx + 4) % 4, (yb - dy + 4) % 4
        return layer * 16 + tx % 2 + 2 * (ty % 2) + 4 * (tx // 2) + 8 * (ty // 2)

    def wait_for(ref, sem):
        pltpu.make_async_copy(ref, ref, sem).wait()

    barrier = pltpu.get_barrier_semaphore()

    def greet(t, carry):
        off = far_first(t)
        for to in (device((mx + off) % NX, my), device(mx, (my + off) % 8)):
            pl.semaphore_signal(barrier, inc=1, device_id=to, device_id_type=MESH)
        return carry

    lax.fori_loop(0, NX - 1, greet, 0)
    for m in TURNS:
        pl.semaphore_signal(barrier, inc=1, device_id=(neighbour(m), me), device_id_type=MESH)

    loads = [
        pltpu.make_async_copy(src, dst, load_sem.at[i])
        for i, (src, dst) in enumerate(
            [
                (child_hbm, child_v),
                (angle_hbm, angle_v),
                (nidx_hbm, nidx_v),
                (ntr_hbm, ntr_v),
                (interp_hbm.at[:, half], interp_v),
                (trans_hbm, trans_v),
            ]
        )
    ]
    for load in loads:
        load.start()

    loads[0].wait()
    for h in range(2):
        block = child_v[h * LANES : (h + 1) * LANES, :].astype(F32)
        send_a[:, h] = block.T.reshape(NX, 16, LANES).astype(BF16)

    pl.semaphore_wait(barrier, 2 * (NX - 1) + len(TURNS))

    def send_child(t, carry):
        to = (mx + far_first(t)) % NX
        pltpu.make_async_remote_copy(
            src_ref=send_a.at[to], dst_ref=recv_a.at[mx],
            send_sem=send_sem.at[0], recv_sem=recv_sem.at[0],
            device_id=device(to, my), device_id_type=MESH,
        ).start()
        return carry

    lax.fori_loop(0, NX - 1, send_child, 0)
    recv_a[mx] = send_a[mx]

    loads[1].wait()
    cos_v[...] = jnp.cos(angle_v[...])
    sin_v[...] = jnp.sin(angle_v[...])

    loads[2].wait()
    loads[3].wait()
    lane = lax.broadcasted_iota(jnp.int32, (32, LANES), 1)

    def mine(ref):
        parts = jnp.zeros((32, LANES), jnp.int32)
        for q in range(LAYERS):
            at = pl.multiple_of(q * 256 + (zc // 8) * LANES, LANES)
            cols = jnp.concatenate(
                [ref[:, pl.ds(at, LANES)], jnp.zeros((32 - NBR, LANES), jnp.int32)], axis=0
            )
            cols = pltpu.roll(cols, (q * BLK - (zc % 8) * BLK + LANES) % LANES, 1)
            parts = jnp.where(lane // BLK == q, cols, parts)
        return parts

    def to_rows(values, at):
        padded = jnp.concatenate([values.astype(F32), jnp.zeros((LANES - 32, LANES), F32)], axis=0)
        rows_v[at] = padded.T[0:GROUP, :]
        return jnp.concatenate([rows_v[at, pl.ds(i, GROUP // 2, stride=2), :] for i in range(2)], axis=0)

    source = mine(nidx_v)
    sx = source % 2 + 2 * ((source // 4) % 2) + 4 * ((source // 16) % 2) + 8 * ((source // 64) % 2)
    sy = (source // 2) % 2 + 2 * ((source // 8) % 2) + 4 * ((source // 32) % 2) + 8 * ((source // 128) % 2)
    sl = source // 256
    u = (sx - 4 * xb + 20) % 16
    v = (sy - 4 * yb + 20) % 16
    bx, x, by, y = u // 4, u % 4, v // 4, v % 4
    turn = by * 3 + bx
    base = GROUP + EDGE * (turn - (turn > 4).astype(jnp.int32))
    by_y = base + 16 * (y - (by == 0).astype(jnp.int32)) + 4 * x + sl
    by_x = base + 16 * (x - (bx == 0).astype(jnp.int32)) + 4 * y + sl
    row = jnp.where(by != 1, by_y, jnp.where(bx != 1, by_x, 16 * y + 4 * x + sl))
    source_rows = to_rows(row, 0)
    factor_rows = to_rows(mine(ntr_v), 1)

    slot_no = lax.broadcasted_iota(jnp.int32, (GROUP, HALO_PAD), 1).astype(F32)
    for n in range(NBR):
        pick_v[n * GROUP : (n + 1) * GROUP, :] = jnp.where(
            source_rows[:, n : n + 1] == slot_no, 1.0, 0.0
        ).astype(BF16)

    new = lax.broadcasted_iota(jnp.int32, (LANES, LANES), 0)
    old = lax.broadcasted_iota(jnp.int32, (LANES, LANES), 1)
    child_out_of = jnp.where((old % 8) * 16 + old // 8 == new, 1.0, 0.0).astype(BF16)
    child_into = jnp.where((new % 8) * 16 + new // 8 == old, 1.0, 0.0).astype(BF16)

    loads[4].wait()
    wait_for(recv_a.at[pl.ds(0, NX - 1)], recv_sem.at[0])
    columns = []
    for g in range(2):
        rows = [None] * 8
        for h in range(2):
            tiles = swap_lane_blocks([recv_a[4 * g + i, h].astype(F32) for i in range(4)])
            for c in range(RHS):
                rows[c * 2 + h] = tiles[c].astype(BF16)
        columns.append(jnp.concatenate(rows, axis=0))
    lhs_v[...] = jnp.dot(
        child_out_of, jnp.concatenate(columns, axis=1), preferred_element_type=F32
    ).astype(BF16)
    interp = interp_v[...].reshape(NCD // 2, NPD)
    for d2 in range(NDIR // 2):
        prod = jnp.dot(
            lhs_v[...], interp[:, d2 * 256 : (d2 + 1) * 256], preferred_element_type=F32
        )
        for i in range(2):
            d = d2 * 2 + i
            at = slice(d * LANES, (d + 1) * LANES)
            for w in range(2):
                by_cos = jnp.zeros((8, LANES), F32)
                by_sin = jnp.zeros((8, LANES), F32)
                for o in range(8):
                    part = prod[o * 16 + w * 8 : o * 16 + w * 8 + 8, i * LANES : (i + 1) * LANES]
                    by_cos = by_cos + part * cos_v[o : o + 1, at]
                    by_sin = by_sin + part * sin_v[o : o + 1, at]
                shifted = by_cos + swap_parts(by_sin, -1.0)
                for c in range(2):
                    send_p[d * RHS + w * 2 + c] = shifted[c * 4 : c * 4 + 4, :]

    my_slot = half * 32 + ((mx % 2 + 2 * (mx // 4)) * 2 + (mx // 2) % 2) * 4 + layer

    def target(t):
        return (mx + far_first(t // 8)) % NX, (my + far_first(t % 8)) % 8

    def send_parent(t, carry):
        tx, ty = target(t)
        pltpu.make_async_remote_copy(
            src_ref=send_p.at[(tx * 2 + ty // 4) * RHS + ty % 4], dst_ref=recv_p.at[my_slot],
            send_sem=send_sem.at[1], recv_sem=recv_sem.at[1],
            device_id=device(tx, ty), device_id_type=MESH,
        ).start()
        return carry

    lax.fori_loop(0, PLANE - 1, send_parent, 0)
    recv_p[my_slot] = send_p[me * RHS + layer]

    loads[5].wait()
    for h in range(2):
        values = trans_v[:, h, :]
        hi = values.astype(BF16)
        lo = (values - hi.astype(F32)).astype(BF16)
        pad = jnp.zeros((NT_PAD - NT, LANES), BF16)
        table_hi[:, h * LANES : (h + 1) * LANES] = jnp.concatenate([hi, pad], axis=0)
        table_lo[:, h * LANES : (h + 1) * LANES] = jnp.concatenate([lo, pad], axis=0)
    field_v[HALO:HALO_PAD, :] = jnp.zeros((HALO_PAD - HALO, 2 * LANES), BF16)

    wait_for(recv_p.at[pl.ds(0, PLANE - 1)], recv_sem.at[1])
    sum_v[...] = recv_p[0:32] + recv_p[32:64]
    for h in range(2):
        cols = slice(h * LANES, (h + 1) * LANES)

        def parents(gx, gy, h=h):
            first = (gy * 2 + gx // 2) * 4
            return sum_v[first : first + 4, h * 2 + gx % 2, :]

        field_v[0:GROUP, cols] = jnp.concatenate(
            [parents(gx, gy) for gy in range(4) for gx in range(4)], axis=0
        ).astype(BF16)
        turned_v[:, cols] = jnp.concatenate(
            [parents(gx, gy) for gx in range(4) for gy in range(4)], axis=0
        ).astype(BF16)

    for k, m in enumerate(TURNS):
        dx, dy = m % 3 - 1, m // 3 - 1
        first = 16 if (dy if dy else dx) < 0 else 0
        pltpu.make_async_remote_copy(
            src_ref=(field_v if dy else turned_v).at[pl.ds(first, EDGE)],
            dst_ref=field_v.at[pl.ds(GROUP + EDGE * k, EDGE)],
            send_sem=send_sem.at[2], recv_sem=recv_sem.at[2],
            device_id=(neighbour(m), me), device_id_type=MESH,
        ).start()

    factor_no = lax.broadcasted_iota(jnp.int32, (GROUP, NT_PAD), 1).astype(F32)
    for s in range(0, NBR, STEP):
        chosen = jnp.concatenate(
            [
                jnp.where(factor_rows[:, n : n + 1] == factor_no, 1.0, 0.0).astype(BF16)
                for n in range(s, s + STEP)
            ],
            axis=0,
        )
        factor_v[s * GROUP : (s + STEP) * GROUP, :] = jnp.dot(
            chosen, table_hi[...], preferred_element_type=F32
        ) + jnp.dot(chosen, table_lo[...], preferred_element_type=F32)

    wait_for(field_v.at[pl.ds(GROUP, 8 * EDGE)], recv_sem.at[2])
    sum_re = jnp.zeros((GROUP, LANES), F32)
    sum_im = jnp.zeros((GROUP, LANES), F32)
    for s in range(0, NBR, STEP):
        picked = jnp.dot(
            pick_v[s * GROUP : (s + STEP) * GROUP, :], field_v[...], preferred_element_type=F32
        )
        for n in range(STEP):
            re = picked[n * GROUP : (n + 1) * GROUP, 0:LANES]
            im = picked[n * GROUP : (n + 1) * GROUP, LANES : 2 * LANES]
            at = (s + n) * GROUP
            t_re = factor_v[at : at + GROUP, 0:LANES]
            t_im = factor_v[at : at + GROUP, LANES : 2 * LANES]
            sum_re = sum_re + (re * t_re - im * t_im)
            sum_im = sum_im + (re * t_im + im * t_re)
    for h, total in enumerate((sum_re, sum_im)):
        total = total.astype(BF16).astype(F32)
        for i in range(2):
            send_q[:, h * 2 + i, :] = total[i * 32 : (i + 1) * 32, :]

    my_piece = me * RHS + layer

    def send_sum(t, carry):
        tx, ty = target(t)
        pltpu.make_async_remote_copy(
            src_ref=send_q.at[(ty % 4) * NX + tx], dst_ref=recv_q.at[my_piece],
            send_sem=send_sem.at[3], recv_sem=recv_sem.at[3],
            device_id=device(tx, ty), device_id_type=MESH,
        ).start()
        return carry

    lax.fori_loop(0, PLANE - 1, send_sum, 0)
    recv_q[my_piece] = send_q[layer * NX + mx]

    wait_for(recv_q.at[pl.ds(0, PLANE - 1)], recv_sem.at[3])
    for d in range(NDIR):
        at = slice(d * LANES, (d + 1) * LANES)
        fields = []
        for w in range(2):
            first = d * RHS + 2 * w
            field = jnp.concatenate([recv_q[first], recv_q[first + 1]], axis=0)
            fields.append((field, swap_parts(field, 1.0)))
        for o in range(8):
            cosine = cos_v[o : o + 1, at]
            sine = sin_v[o : o + 1, at]
            back_v[o * 16 : (o + 1) * 16, at] = jnp.concatenate(
                [field * cosine + turned * sine for field, turned in fields], axis=0
            ).astype(BF16)
    prod = 0.125 * lax.dot_general(
        back_v[...], interp, (((1,), (1,)), ((), ())), preferred_element_type=F32
    )
    prod = jnp.dot(child_into, prod.astype(BF16), preferred_element_type=F32)
    for g in range(2):
        for h in range(2):
            tiles = swap_lane_blocks(
                [
                    prod[c * 32 + h * 16 : c * 32 + h * 16 + 16, g * LANES : (g + 1) * LANES]
                    for c in range(RHS)
                ]
            )
            for i in range(4):
                send_c[4 * g + i, h] = tiles[i].astype(BF16)

    def send_result(t, carry):
        to = (mx + far_first(t)) % NX
        pltpu.make_async_remote_copy(
            src_ref=send_c.at[to], dst_ref=recv_c.at[mx],
            send_sem=send_sem.at[4], recv_sem=recv_sem.at[4],
            device_id=device(to, my), device_id_type=MESH,
        ).start()
        return carry

    lax.fori_loop(0, NX - 1, send_result, 0)
    recv_c[mx] = send_c[mx]
    wait_for(recv_c.at[pl.ds(0, NX - 1)], recv_sem.at[4])
    for h in range(2):
        block = recv_c[:, h].astype(F32).reshape(LANES, LANES)
        out_ref[h * LANES : (h + 1) * LANES, :] = block.T.astype(BF16)

    wait_for(send_a.at[pl.ds(0, NX - 1)], send_sem.at[0])
    wait_for(send_p.at[pl.ds(0, PLANE - 1)], send_sem.at[1])
    wait_for(field_v.at[pl.ds(0, 8 * EDGE)], send_sem.at[2])
    wait_for(recv_q.at[pl.ds(0, PLANE - 1)], send_sem.at[3])
    wait_for(send_c.at[pl.ds(0, NX - 1)], send_sem.at[4])


def per_device(child_out, interp, shift_angle, translators, nbr_index, nbr_trans):
    count, cols, width = child_out.shape
    children = child_out.transpose(1, 2, 0).reshape(cols * width, count)
    out = pl.pallas_call(
        kernel,
        out_shape=jax.ShapeDtypeStruct((cols * width, count), BF16),
        in_specs=[pl.BlockSpec(memory_space=pl.ANY)] * 6,
        out_specs=pl.BlockSpec(memory_space=pltpu.VMEM),
        scratch_shapes=[
            pltpu.VMEM((cols * width, count), BF16),
            pltpu.VMEM((NX, 32, NPD), BF16),
            pltpu.VMEM((8, NPD), F32),
            pltpu.VMEM((NT, 2, LANES), F32),
            pltpu.VMEM((NBR, 1024), jnp.int32),
            pltpu.VMEM((NBR, 1024), jnp.int32),
            pltpu.VMEM((NX, 2, 16, LANES), BF16),
            pltpu.VMEM((NX, 2, 16, LANES), BF16),
            pltpu.VMEM((LANES, NCD // 2), BF16),
            pltpu.VMEM((8, NPD), F32),
            pltpu.VMEM((8, NPD), F32),
            pltpu.VMEM((PLANE, 4, LANES), F32),
            pltpu.VMEM((PLANE, 4, LANES), F32),
            pltpu.VMEM((PLANE // 2, 4, LANES), F32),
            pltpu.VMEM((HALO_PAD, 2 * LANES), BF16),
            pltpu.VMEM((GROUP, 2 * LANES), BF16),
            pltpu.VMEM((2, GROUP, LANES), F32),
            pltpu.VMEM((NBR * GROUP, HALO_PAD), BF16),
            pltpu.VMEM((NBR * GROUP, 2 * LANES), F32),
            pltpu.VMEM((NT_PAD, 2 * LANES), BF16),
            pltpu.VMEM((NT_PAD, 2 * LANES), BF16),
            pltpu.VMEM((PLANE // 2, 4, LANES), F32),
            pltpu.VMEM((PLANE, 4, LANES), F32),
            pltpu.VMEM((LANES, NPD), BF16),
            pltpu.VMEM((NX, 2, 16, LANES), BF16),
            pltpu.VMEM((NX, 2, 16, LANES), BF16),
            pltpu.SemaphoreType.DMA((6,)),
            pltpu.SemaphoreType.DMA((5,)),
            pltpu.SemaphoreType.DMA((5,)),
        ],
        compiler_params=pltpu.CompilerParams(
            collective_id=0, has_side_effects=True, vmem_limit_bytes=60 * 1024 * 1024
        ),
    )(
        children,
        interp.reshape(NX, 2, 32, NPD),
        shift_angle,
        translators,
        nbr_index.T,
        nbr_trans.T,
    )
    return out.reshape(cols, width, count).transpose(2, 0, 1)


def solution(mesh):
    return jax.shard_map(
        per_device,
        mesh=mesh,
        in_specs=(P("box", None, "dir"), P(), P(), P(None, None, "dir"), P(), P()),
        out_specs=P("box", None, "dir"),
        check_vma=False,
    )
```

```python
import jax
import jax.numpy as jnp
from jax import lax
from jax.experimental import pallas as pl
from jax.experimental.pallas import tpu as pltpu
from jax.sharding import PartitionSpec as P

MESH = pl.DeviceIdType.MESH
F32 = jnp.float32
BF16 = jnp.bfloat16

NCD = 512
NPD = 2048
NBR = 27
NT = 343
NX = 8
NY = 8
WIDE = NPD // 2
RHS = 4
LAYERS = 4
BLK = 16
LANES = 128
GROUP = LAYERS * BLK
EDGE = 48
HALO = GROUP + 8 * EDGE
HALO_PAD = 512
NT_SENT = 352
NT_PAD = 384
STEP = 9
TURNS = [m for m in range(9) if m != 4]


def far_first(s):
    return 4 + (1 - 2 * (s % 2)) * ((s + 1) // 2)


def kernel(
    child_hbm, interp_hbm, angle_hbm, trans_hbm, nidx_hbm, ntr_hbm, out_ref,
    interp_v, angle_v, trans_v, nidx_v, ntr_v,
    recv_a, cos_v, sin_v, table_out, table_v, send_b, recv_b, field_v, turned_v,
    pick_v, factor_v, send_d, recv_d, parent_v, back_v, send_e, recv_e,
    load_sem, send_sem, recv_sem,
):
    box = lax.axis_index("box")
    me = lax.axis_index("dir")
    layer = box // 16
    zc = box % 16
    xb = zc % 2 + 2 * ((zc // 4) % 2)
    yb = (zc // 2) % 2 + 2 * (zc // 8)
    mx = me // 2
    half = me % 2
    my = half * 4 + layer

    def device(x, y):
        return ((y % 4) * 16 + zc, x * 2 + y // 4)

    def neighbour(m):
        dx, dy = m % 3 - 1, m // 3 - 1
        tx, ty = (xb - dx + 4) % 4, (yb - dy + 4) % 4
        return layer * 16 + tx % 2 + 2 * (ty % 2) + 4 * (tx // 2) + 8 * (ty // 2)

    def wait_for(ref, sem):
        pltpu.make_async_copy(ref, ref, sem).wait()

    def send(src, dst, phase, to):
        return pltpu.make_async_remote_copy(
            src_ref=src, dst_ref=dst, send_sem=send_sem.at[phase], recv_sem=recv_sem.at[phase],
            device_id=to, device_id_type=MESH,
        )

    barrier = pltpu.get_barrier_semaphore()

    def greet(t, carry):
        off = far_first(t)
        for to in (device((mx + off) % NX, my), device(mx, (my + off) % NY)):
            pl.semaphore_signal(barrier, inc=1, device_id=to, device_id_type=MESH)
        return carry

    lax.fori_loop(0, NX - 1, greet, 0)
    for m in TURNS:
        pl.semaphore_signal(barrier, inc=1, device_id=(neighbour(m), me), device_id_type=MESH)

    copies = [
        (child_hbm.at[:, mx % 4], recv_a.at[mx]),
        (trans_hbm, trans_v),
        (nidx_hbm, nidx_v),
        (ntr_hbm, ntr_v),
    ]
    for q in range(LAYERS):
        at = pl.ds(pl.multiple_of((mx + 7 + q) % NX * 256, 256), 256)
        to = pl.ds(q * 256, 256)
        copies.append((angle_hbm.at[:, at], angle_v.at[:, to]))
        copies.append((interp_hbm.at[:, half, :, at], interp_v.at[:, :, to]))
    loads = [pltpu.make_async_copy(src, dst, load_sem.at[i]) for i, (src, dst) in enumerate(copies)]
    for load in loads:
        load.start()

    pl.semaphore_wait(barrier, (NX - 1) + (NY - 1) + len(TURNS))

    def send_child(t, carry):
        to = (mx + far_first(t)) % NX
        send(child_hbm.at[:, to % 4], recv_a.at[mx], 0, device(to, my)).start()
        return carry

    lax.fori_loop(0, NX - 1, send_child, 0)

    loads[1].wait()
    for h in range(2):
        table_out[:, h * LANES : (h + 1) * LANES] = jnp.concatenate(
            [trans_v[:, h, :], jnp.zeros((NT_SENT - NT, LANES), F32)], axis=0
        ).astype(BF16)
    table_v[NT_SENT:NT_PAD, :] = jnp.zeros((NT_PAD - NT_SENT, 2 * LANES), BF16)
    table_in = table_v.at[pl.ds(0, NT_SENT)]
    send_table = send(table_out, table_in, 5, device((mx + 9 - layer) % NX, my))

    @pl.when(layer != 1)
    def _():
        send_table.start()

    @pl.when(layer == 1)
    def _():
        pltpu.make_async_copy(table_out, table_in, recv_sem.at[5]).start()

    for q in range(LAYERS):
        loads[4 + 2 * q].wait()
    cos_v[...] = jnp.cos(angle_v[...])
    sin_v[...] = jnp.sin(angle_v[...])

    loads[2].wait()
    loads[3].wait()
    lane = lax.broadcasted_iota(jnp.int32, (32, LANES), 1)

    def mine(ref):
        parts = jnp.zeros((32, LANES), jnp.int32)
        for q in range(LAYERS):
            at = pl.multiple_of(q * 256 + (zc // 8) * LANES, LANES)
            cols = jnp.concatenate(
                [ref[:, pl.ds(at, LANES)], jnp.zeros((32 - NBR, LANES), jnp.int32)], axis=0
            )
            cols = pltpu.roll(cols, (q * BLK - (zc % 8) * BLK + LANES) % LANES, 1)
            parts = jnp.where(lane // BLK == q, cols, parts)
        return parts

    source = mine(nidx_v)
    sx = source % 2 + 2 * ((source // 4) % 2) + 4 * ((source // 16) % 2) + 8 * ((source // 64) % 2)
    sy = (source // 2) % 2 + 2 * ((source // 8) % 2) + 4 * ((source // 32) % 2) + 8 * ((source // 128) % 2)
    sl = source // 256
    u = (sx - 4 * xb + 20) % 16
    v = (sy - 4 * yb + 20) % 16
    bx, x, by, y = u // 4, u % 4, v // 4, v % 4
    turn = by * 3 + bx
    base = GROUP + EDGE * (turn - (turn > 4).astype(jnp.int32))
    by_y = base + 16 * (y - (by == 0).astype(jnp.int32)) + 4 * x + sl
    by_x = base + 16 * (x - (bx == 0).astype(jnp.int32)) + 4 * y + sl
    row = jnp.where(by != 1, by_y, jnp.where(bx != 1, by_x, 16 * y + 4 * x + sl))
    source_rows = row.astype(F32).T[0:GROUP, :]
    factor_rows = mine(ntr_v).astype(F32).T[0:GROUP, :]

    slot_no = lax.broadcasted_iota(jnp.int32, (GROUP, HALO_PAD), 1).astype(F32)
    for n in range(NBR):
        pick_v[n * GROUP : (n + 1) * GROUP, :] = jnp.where(
            source_rows[:, n : n + 1] == slot_no, 1.0, 0.0
        ).astype(BF16)
    field_v[HALO:HALO_PAD, :] = jnp.zeros((HALO_PAD - HALO, 2 * LANES), BF16)

    new = lax.broadcasted_iota(jnp.int32, (LANES, LANES), 0)
    old = lax.broadcasted_iota(jnp.int32, (LANES, LANES), 1)
    by_child = jnp.where((old % 8) * 16 + old // 8 == new, 1.0, 0.0).astype(BF16)
    new = lax.broadcasted_iota(jnp.int32, (2 * GROUP, GROUP), 0)
    old = lax.broadcasted_iota(jnp.int32, (2 * GROUP, GROUP), 1)
    px = old % 2 + 2 * ((old // 4) % 2)
    py = (old // 2) % 2 + 2 * ((old // 8) % 2)
    straight = 16 * py + 4 * px + old // 16
    turned = GROUP + 16 * px + 4 * py + old // 16
    in_order = jnp.where((straight == new) | (turned == new), 1.0, 0.0).astype(BF16)

    for q in range(LAYERS):
        loads[5 + 2 * q].wait()
    loads[0].wait()
    wait_for(recv_a.at[pl.ds(0, NX - 1)], recv_sem.at[0])
    children = jnp.concatenate(
        [
            lax.dot_general(
                by_child, recv_a[:, h].reshape(NCD // 2, LANES), (((1,), (1,)), ((), ())),
                preferred_element_type=F32,
            ).astype(BF16)
            for h in range(2)
        ],
        axis=0,
    )
    interp = interp_v[...].reshape(NCD // 2, WIDE)
    for q in range(LAYERS):
        prod = jnp.dot(
            children, interp[:, q * 256 : (q + 1) * 256], preferred_element_type=F32
        )
        for i in range(2):
            at = slice(q * 256 + i * LANES, q * 256 + (i + 1) * LANES)
            total_re = jnp.zeros((BLK, LANES), F32)
            total_im = jnp.zeros((BLK, LANES), F32)
            for o in range(8):
                re = prod[o * BLK : (o + 1) * BLK, i * LANES : (i + 1) * LANES]
                im = prod[LANES + o * BLK : LANES + (o + 1) * BLK, i * LANES : (i + 1) * LANES]
                cosine = cos_v[o : o + 1, at]
                sine = sin_v[o : o + 1, at]
                total_re = total_re + (re * cosine - im * sine)
                total_im = total_im + (re * sine + im * cosine)
            send_b[i * 4 + q, 0] = total_re.astype(BF16)
            send_b[i * 4 + q, 1] = total_im.astype(BF16)

            @pl.when(i * 4 + q != my)
            def _(to=i * 4 + q):
                send(send_b.at[to], recv_b.at[my], 1, device(mx, to)).start()

    recv_b[my] = send_b[my]

    wait_for(recv_b.at[pl.ds(0, NY - 1)], recv_sem.at[1])
    whole = (recv_b[0:4].astype(F32) + recv_b[4:8].astype(F32)).astype(BF16)
    whole = jnp.concatenate([whole[:, h].reshape(GROUP, LANES) for h in range(2)], axis=1)
    ordered = jnp.dot(in_order, whole, preferred_element_type=F32).astype(BF16)
    field_v[0:GROUP, :] = ordered[0:GROUP]
    turned_v[...] = ordered[GROUP : 2 * GROUP]

    for k, m in enumerate(TURNS):
        dx, dy = m % 3 - 1, m // 3 - 1
        first = 16 if (dy if dy else dx) < 0 else 0
        send(
            (field_v if dy else turned_v).at[pl.ds(first, EDGE)],
            field_v.at[pl.ds(GROUP + EDGE * k, EDGE)],
            2,
            (neighbour(m), me),
        ).start()

    wait_for(table_in, recv_sem.at[5])
    factor_no = lax.broadcasted_iota(jnp.int32, (GROUP, NT_PAD), 1).astype(F32)
    for s in range(0, NBR, STEP):
        chosen = jnp.concatenate(
            [
                jnp.where(factor_rows[:, n : n + 1] == factor_no, 1.0, 0.0).astype(BF16)
                for n in range(s, s + STEP)
            ],
            axis=0,
        )
        factor_v[s * GROUP : (s + STEP) * GROUP, :] = jnp.dot(
            chosen, table_v[...], preferred_element_type=F32
        )

    wait_for(field_v.at[pl.ds(GROUP, 8 * EDGE)], recv_sem.at[2])
    sum_re = jnp.zeros((GROUP, LANES), F32)
    sum_im = jnp.zeros((GROUP, LANES), F32)
    for s in range(0, NBR, STEP):
        picked = jnp.dot(
            pick_v[s * GROUP : (s + STEP) * GROUP, :], field_v[...], preferred_element_type=F32
        )
        for n in range(STEP):
            re = picked[n * GROUP : (n + 1) * GROUP, 0:LANES]
            im = picked[n * GROUP : (n + 1) * GROUP, LANES : 2 * LANES]
            at = (s + n) * GROUP
            t_re = factor_v[at : at + GROUP, 0:LANES]
            t_im = factor_v[at : at + GROUP, LANES : 2 * LANES]
            sum_re = sum_re + (re * t_re - im * t_im)
            sum_im = sum_im + (re * t_im + im * t_re)
    for h, total in enumerate((sum_re, sum_im)):
        send_d[:, h] = total.astype(BF16).reshape(LAYERS, BLK, LANES)

    def send_sum(t, carry):
        to = (my + far_first(t)) % NY
        send(send_d.at[to % 4], recv_d.at[my], 3, device(mx, to)).start()
        return carry

    lax.fori_loop(0, NY - 1, send_sum, 0)
    recv_d[my] = send_d[layer]

    wait_for(recv_d.at[pl.ds(0, NY - 1)], recv_sem.at[3])
    parent_v[...] = recv_d[...].astype(F32)
    for i in range(2):
        for q in range(LAYERS):
            at = slice(q * 256 + i * LANES, q * 256 + (i + 1) * LANES)
            cosine = cos_v[:, at]
            sine = sin_v[:, at]
            for p in range(0, BLK, 2):
                backs = [[], []]
                for r in range(p, p + 2):
                    re = parent_v[i * 4 + q, 0, r : r + 1, :]
                    im = parent_v[i * 4 + q, 1, r : r + 1, :]
                    backs[0].append(re * cosine + im * sine)
                    backs[1].append(im * cosine - re * sine)
                for h in range(2):
                    first = h * LANES + p * 8
                    back_v[first : first + 16, at] = jnp.concatenate(backs[h], axis=0).astype(BF16)
    prod = 0.125 * lax.dot_general(
        interp, back_v[...], (((1,), (1,)), ((), ())), preferred_element_type=F32
    )
    for h in range(2):
        send_e[:, h] = prod[:, h * LANES : (h + 1) * LANES].astype(BF16).reshape(NX, 32, LANES)

    def send_result(t, carry):
        to = (mx + far_first(t)) % NX
        send(send_e.at[to], recv_e.at[mx], 4, device(to, my)).start()
        return carry

    lax.fori_loop(0, NX - 1, send_result, 0)
    recv_e[mx] = send_e[mx]
    wait_for(recv_e.at[pl.ds(0, NX - 1)], recv_sem.at[4])
    for h in range(2):
        for c in range(RHS):
            first = h * LANES + c * 32
            out_ref[first : first + 32, :] = (
                recv_e[c, h].astype(F32) + recv_e[c + 4, h].astype(F32)
            ).astype(BF16)

    wait_for(recv_a.at[pl.ds(0, NX - 1)], send_sem.at[0])
    wait_for(send_b.at[pl.ds(0, NY - 1)], send_sem.at[1])
    wait_for(field_v.at[pl.ds(0, 8 * EDGE)], send_sem.at[2])
    wait_for(recv_d.at[pl.ds(0, NY - 1)], send_sem.at[3])
    wait_for(send_e.at[pl.ds(0, NX - 1)], send_sem.at[4])

    @pl.when(layer != 1)
    def _():
        wait_for(table_out, send_sem.at[5])


def per_device(child_out, interp, shift_angle, translators, nbr_index, nbr_trans):
    count, cols, width = child_out.shape
    children = child_out.transpose(1, 2, 0).reshape(2, RHS, width, count)
    out = pl.pallas_call(
        kernel,
        out_shape=jax.ShapeDtypeStruct((cols * width, count), BF16),
        in_specs=[pl.BlockSpec(memory_space=pl.ANY)] * 6,
        out_specs=pl.BlockSpec(memory_space=pltpu.VMEM),
        scratch_shapes=[
            pltpu.VMEM((NX, 32, WIDE), BF16),
            pltpu.VMEM((8, WIDE), F32),
            pltpu.VMEM((NT, 2, LANES), F32),
            pltpu.VMEM((NBR, 1024), jnp.int32),
            pltpu.VMEM((NBR, 1024), jnp.int32),
            pltpu.VMEM((NX, 2, 32, LANES), BF16),
            pltpu.VMEM((8, WIDE), F32),
            pltpu.VMEM((8, WIDE), F32),
            pltpu.VMEM((NT_SENT, 2 * LANES), BF16),
            pltpu.VMEM((NT_PAD, 2 * LANES), BF16),
            pltpu.VMEM((NY, 2, BLK, LANES), BF16),
            pltpu.VMEM((NY, 2, BLK, LANES), BF16),
            pltpu.VMEM((HALO_PAD, 2 * LANES), BF16),
            pltpu.VMEM((GROUP, 2 * LANES), BF16),
            pltpu.VMEM((NBR * GROUP, HALO_PAD), BF16),
            pltpu.VMEM((NBR * GROUP, 2 * LANES), F32),
            pltpu.VMEM((LAYERS, 2, BLK, LANES), BF16),
            pltpu.VMEM((NY, 2, BLK, LANES), BF16),
            pltpu.VMEM((NY, 2, BLK, LANES), F32),
            pltpu.VMEM((2 * LANES, WIDE), BF16),
            pltpu.VMEM((NX, 2, 32, LANES), BF16),
            pltpu.VMEM((NX, 2, 32, LANES), BF16),
            pltpu.SemaphoreType.DMA((12,)),
            pltpu.SemaphoreType.DMA((6,)),
            pltpu.SemaphoreType.DMA((6,)),
        ],
        compiler_params=pltpu.CompilerParams(
            collective_id=0, has_side_effects=True, vmem_limit_bytes=60 * 1024 * 1024
        ),
    )(
        children,
        interp.reshape(NX, 2, 32, NPD),
        shift_angle,
        translators,
        nbr_index.T,
        nbr_trans.T,
    )
    return out.reshape(cols, width, count).transpose(2, 0, 1)


def solution(mesh):
    return jax.shard_map(
        per_device,
        mesh=mesh,
        in_specs=(P("box", None, "dir"), P(), P(), P(None, None, "dir"), P(), P()),
        out_specs=P("box", None, "dir"),
        check_vma=False,
    )
```

```python
import jax
import jax.numpy as jnp
from jax import lax
from jax.experimental import pallas as pl
from jax.experimental.pallas import tpu as pltpu
from jax.sharding import PartitionSpec as P

MESH = pl.DeviceIdType.MESH
F32 = jnp.float32
BF16 = jnp.bfloat16

NCD = 512
NPD = 2048
NBR = 27
NT = 343
NX = 8
NY = 8
WIDE = NPD // 2
RHS = 4
LAYERS = 4
BLK = 16
LANES = 128
GROUP = LAYERS * BLK
EDGE = 48
HALO = GROUP + 8 * EDGE
HALO_PAD = 512
NT_SENT = 352
NT_PAD = 384
STEP = 9
TURNS = [m for m in range(9) if m != 4]


def far_first(s):
    return 4 + (1 - 2 * (s % 2)) * ((s + 1) // 2)


def kernel(
    child_hbm, interp_hbm, angle_hbm, trans_hbm, nidx_hbm, ntr_hbm, out_ref,
    child_v, interp_v, angle_v, trans_v, nidx_v, ntr_v,
    recv_a, cos_v, sin_v, table_out, table_v, send_b, recv_b, field_v, turned_v,
    pick_v, factor_v, send_d, recv_d, parent_v, back_v, send_e, recv_e,
    load_sem, send_sem, recv_sem,
):
    box = lax.axis_index("box")
    me = lax.axis_index("dir")
    layer = box // 16
    zc = box % 16
    xb = zc % 2 + 2 * ((zc // 4) % 2)
    yb = (zc // 2) % 2 + 2 * (zc // 8)
    mx = me // 2
    half = me % 2
    my = half * 4 + layer

    def device(x, y):
        return ((y % 4) * 16 + zc, x * 2 + y // 4)

    def neighbour(m):
        dx, dy = m % 3 - 1, m // 3 - 1
        tx, ty = (xb - dx + 4) % 4, (yb - dy + 4) % 4
        return layer * 16 + tx % 2 + 2 * (ty % 2) + 4 * (tx // 2) + 8 * (ty // 2)

    def wait_for(ref, sem):
        pltpu.make_async_copy(ref, ref, sem).wait()

    def send(src, dst, phase, to):
        return pltpu.make_async_remote_copy(
            src_ref=src, dst_ref=dst, send_sem=send_sem.at[phase], recv_sem=recv_sem.at[phase],
            device_id=to, device_id_type=MESH,
        )

    barrier = pltpu.get_barrier_semaphore()

    def greet(t, carry):
        off = far_first(t)
        for to in (device((mx + off) % NX, my), device(mx, (my + off) % NY)):
            pl.semaphore_signal(barrier, inc=1, device_id=to, device_id_type=MESH)
        return carry

    lax.fori_loop(0, NX - 1, greet, 0)
    for m in TURNS:
        pl.semaphore_signal(barrier, inc=1, device_id=(neighbour(m), me), device_id_type=MESH)

    copies = [
        (child_hbm, child_v),
        (trans_hbm, trans_v),
        (nidx_hbm, nidx_v),
        (ntr_hbm, ntr_v),
    ]
    for q in range(LAYERS):
        at = pl.ds(pl.multiple_of((mx + 7 + q) % NX * 256, 256), 256)
        to = pl.ds(q * 256, 256)
        copies.append((angle_hbm.at[:, at], angle_v.at[:, to]))
        copies.append((interp_hbm.at[:, half, :, at], interp_v.at[:, :, to]))
    loads = [pltpu.make_async_copy(src, dst, load_sem.at[i]) for i, (src, dst) in enumerate(copies)]
    for load in loads:
        load.start()

    loads[0].wait()
    recv_a[mx] = child_v[:, mx % 4]
    pl.semaphore_wait(barrier, (NX - 1) + (NY - 1) + len(TURNS))

    def send_child(t, carry):
        to = (mx + far_first(t)) % NX
        send(child_v.at[:, to % 4], recv_a.at[mx], 0, device(to, my)).start()
        return carry

    lax.fori_loop(0, NX - 1, send_child, 0)

    loads[1].wait()
    for h in range(2):
        table_out[:, h * LANES : (h + 1) * LANES] = jnp.concatenate(
            [trans_v[:, h, :], jnp.zeros((NT_SENT - NT, LANES), F32)], axis=0
        ).astype(BF16)
    table_v[NT_SENT:NT_PAD, :] = jnp.zeros((NT_PAD - NT_SENT, 2 * LANES), BF16)
    table_in = table_v.at[pl.ds(0, NT_SENT)]
    for q in range(LAYERS):
        loads[4 + 2 * q].wait()
    cos_v[...] = jnp.cos(angle_v[...])
    sin_v[...] = jnp.sin(angle_v[...])

    loads[2].wait()
    loads[3].wait()
    lane = lax.broadcasted_iota(jnp.int32, (32, LANES), 1)

    def mine(ref):
        parts = jnp.zeros((32, LANES), jnp.int32)
        for q in range(LAYERS):
            at = pl.multiple_of(q * 256 + (zc // 8) * LANES, LANES)
            cols = jnp.concatenate(
                [ref[:, pl.ds(at, LANES)], jnp.zeros((32 - NBR, LANES), jnp.int32)], axis=0
            )
            cols = pltpu.roll(cols, (q * BLK - (zc % 8) * BLK + LANES) % LANES, 1)
            parts = jnp.where(lane // BLK == q, cols, parts)
        return parts

    source = mine(nidx_v)
    sx = source % 2 + 2 * ((source // 4) % 2) + 4 * ((source // 16) % 2) + 8 * ((source // 64) % 2)
    sy = (source // 2) % 2 + 2 * ((source // 8) % 2) + 4 * ((source // 32) % 2) + 8 * ((source // 128) % 2)
    sl = source // 256
    u = (sx - 4 * xb + 20) % 16
    v = (sy - 4 * yb + 20) % 16
    bx, x, by, y = u // 4, u % 4, v // 4, v % 4
    turn = by * 3 + bx
    base = GROUP + EDGE * (turn - (turn > 4).astype(jnp.int32))
    by_y = base + 16 * (y - (by == 0).astype(jnp.int32)) + 4 * x + sl
    by_x = base + 16 * (x - (bx == 0).astype(jnp.int32)) + 4 * y + sl
    row = jnp.where(by != 1, by_y, jnp.where(bx != 1, by_x, 16 * y + 4 * x + sl))
    source_rows = row.astype(F32).T[0:GROUP, :]
    factor_rows = mine(ntr_v).astype(F32).T[0:GROUP, :]

    slot_no = lax.broadcasted_iota(jnp.int32, (GROUP, HALO_PAD), 1).astype(F32)
    for n in range(NBR):
        pick_v[n * GROUP : (n + 1) * GROUP, :] = jnp.where(
            source_rows[:, n : n + 1] == slot_no, 1.0, 0.0
        ).astype(BF16)
    field_v[HALO:HALO_PAD, :] = jnp.zeros((HALO_PAD - HALO, 2 * LANES), BF16)

    new = lax.broadcasted_iota(jnp.int32, (LANES, LANES), 0)
    old = lax.broadcasted_iota(jnp.int32, (LANES, LANES), 1)
    by_child = jnp.where((old % 8) * 16 + old // 8 == new, 1.0, 0.0).astype(BF16)
    new = lax.broadcasted_iota(jnp.int32, (2 * GROUP, GROUP), 0)
    old = lax.broadcasted_iota(jnp.int32, (2 * GROUP, GROUP), 1)
    px = old % 2 + 2 * ((old // 4) % 2)
    py = (old // 2) % 2 + 2 * ((old // 8) % 2)
    straight = 16 * py + 4 * px + old // 16
    turned = GROUP + 16 * px + 4 * py + old // 16
    in_order = jnp.where((straight == new) | (turned == new), 1.0, 0.0).astype(BF16)

    for q in range(LAYERS):
        loads[5 + 2 * q].wait()
    wait_for(recv_a.at[pl.ds(0, NX - 1)], recv_sem.at[0])
    send_table = send(table_out, table_in, 5, device((mx + 9 - layer) % NX, my))

    @pl.when(layer != 1)
    def _():
        send_table.start()

    @pl.when(layer == 1)
    def _():
        pltpu.make_async_copy(table_out, table_in, recv_sem.at[5]).start()

    children = jnp.concatenate(
        [
            lax.dot_general(
                by_child, recv_a[:, h].reshape(NCD // 2, LANES), (((1,), (1,)), ((), ())),
                preferred_element_type=F32,
            ).astype(BF16)
            for h in range(2)
        ],
        axis=0,
    )
    for turn in (0, 3, 1, 2):
        q = (layer + turn) % LAYERS
        some = interp_v[:, :, pl.ds(pl.multiple_of(q * 256, 256), 256)]
        prod = jnp.dot(children, some.reshape(NCD // 2, 256), preferred_element_type=F32)
        for i in range(2):
            at = pl.ds(pl.multiple_of(q * 256 + i * LANES, LANES), LANES)
            total_re = jnp.zeros((BLK, LANES), F32)
            total_im = jnp.zeros((BLK, LANES), F32)
            for o in range(8):
                re = prod[o * BLK : (o + 1) * BLK, i * LANES : (i + 1) * LANES]
                im = prod[LANES + o * BLK : LANES + (o + 1) * BLK, i * LANES : (i + 1) * LANES]
                cosine = cos_v[pl.ds(o, 1), at]
                sine = sin_v[pl.ds(o, 1), at]
                total_re = total_re + (re * cosine - im * sine)
                total_im = total_im + (re * sine + im * cosine)
            send_b[i * 4 + q, 0] = total_re.astype(BF16)
            send_b[i * 4 + q, 1] = total_im.astype(BF16)

            @pl.when(i * 4 + q != my)
            def _(to=i * 4 + q):
                send(send_b.at[to], recv_b.at[my], 1, device(mx, to)).start()

    recv_b[my] = send_b[my]

    wait_for(recv_b.at[pl.ds(0, NY - 1)], recv_sem.at[1])
    whole = (recv_b[0:4].astype(F32) + recv_b[4:8].astype(F32)).astype(BF16)
    whole = jnp.concatenate([whole[:, h].reshape(GROUP, LANES) for h in range(2)], axis=1)
    ordered = jnp.dot(in_order, whole, preferred_element_type=F32).astype(BF16)
    field_v[0:GROUP, :] = ordered[0:GROUP]
    turned_v[...] = ordered[GROUP : 2 * GROUP]

    for fx, fy in ((3, 3), (0, 3), (1, 3), (3, 1), (3, 0), (0, 1), (1, 1), (1, 0)):
        dx = (1 if fx == 3 else -1) * (1 - 2 * (xb % 2)) if fx else 0
        dy = (1 if fy == 3 else -1) * (1 - 2 * (yb % 2)) if fy else 0
        m = (dy + 1) * 3 + dx + 1
        slot = m - (m + 4) // 9
        first = pl.multiple_of(8 - 8 * (dy if fy else dx), 16)
        at = pl.multiple_of(GROUP + EDGE * slot, 16)
        send(
            (field_v if fy else turned_v).at[pl.ds(first, EDGE)],
            field_v.at[pl.ds(at, EDGE)],
            2,
            (neighbour(m), me),
        ).start()

    wait_for(table_in, recv_sem.at[5])
    factor_no = lax.broadcasted_iota(jnp.int32, (GROUP, NT_PAD), 1).astype(F32)
    for s in range(0, NBR, STEP):
        chosen = jnp.concatenate(
            [
                jnp.where(factor_rows[:, n : n + 1] == factor_no, 1.0, 0.0).astype(BF16)
                for n in range(s, s + STEP)
            ],
            axis=0,
        )
        factor_v[s * GROUP : (s + STEP) * GROUP, :] = jnp.dot(
            chosen, table_v[...], preferred_element_type=F32
        )

    wait_for(field_v.at[pl.ds(GROUP, 8 * EDGE)], recv_sem.at[2])
    sum_re = jnp.zeros((GROUP, LANES), F32)
    sum_im = jnp.zeros((GROUP, LANES), F32)
    for s in range(0, NBR, STEP):
        picked = jnp.dot(
            pick_v[s * GROUP : (s + STEP) * GROUP, :], field_v[...], preferred_element_type=F32
        )
        for n in range(STEP):
            re = picked[n * GROUP : (n + 1) * GROUP, 0:LANES]
            im = picked[n * GROUP : (n + 1) * GROUP, LANES : 2 * LANES]
            at = (s + n) * GROUP
            t_re = factor_v[at : at + GROUP, 0:LANES]
            t_im = factor_v[at : at + GROUP, LANES : 2 * LANES]
            sum_re = sum_re + (re * t_re - im * t_im)
            sum_im = sum_im + (re * t_im + im * t_re)
    for h, total in enumerate((sum_re, sum_im)):
        send_d[:, h] = total.astype(BF16).reshape(LAYERS, BLK, LANES)

    def send_sum(t, carry):
        to = (my + far_first(t)) % NY
        send(send_d.at[to % 4], recv_d.at[my], 3, device(mx, to)).start()
        return carry

    lax.fori_loop(0, NY - 1, send_sum, 0)
    recv_d[my] = send_d[layer]

    wait_for(recv_d.at[pl.ds(0, NY - 1)], recv_sem.at[3])
    parent_v[...] = recv_d[...].astype(F32)
    for i in range(2):
        for q in range(LAYERS):
            at = slice(q * 256 + i * LANES, q * 256 + (i + 1) * LANES)
            cosine = cos_v[:, at]
            sine = sin_v[:, at]
            for p in range(0, BLK, 2):
                backs = [[], []]
                for r in range(p, p + 2):
                    re = parent_v[i * 4 + q, 0, r : r + 1, :]
                    im = parent_v[i * 4 + q, 1, r : r + 1, :]
                    backs[0].append(re * cosine + im * sine)
                    backs[1].append(im * cosine - re * sine)
                for h in range(2):
                    first = h * LANES + p * 8
                    back_v[first : first + 16, at] = jnp.concatenate(backs[h], axis=0).astype(BF16)
    prod = 0.125 * lax.dot_general(
        interp_v[...].reshape(NCD // 2, WIDE), back_v[...], (((1,), (1,)), ((), ())), preferred_element_type=F32
    )
    for h in range(2):
        send_e[:, h] = prod[:, h * LANES : (h + 1) * LANES].astype(BF16).reshape(NX, 32, LANES)

    def send_result(t, carry):
        to = (mx + far_first(t)) % NX
        send(send_e.at[to], recv_e.at[mx], 4, device(to, my)).start()
        return carry

    lax.fori_loop(0, NX - 1, send_result, 0)
    recv_e[mx] = send_e[mx]
    wait_for(recv_e.at[pl.ds(0, NX - 1)], recv_sem.at[4])
    for h in range(2):
        for c in range(RHS):
            first = h * LANES + c * 32
            out_ref[first : first + 32, :] = (
                recv_e[c, h].astype(F32) + recv_e[c + 4, h].astype(F32)
            ).astype(BF16)

    wait_for(recv_a.at[pl.ds(0, NX - 1)], send_sem.at[0])
    wait_for(send_b.at[pl.ds(0, NY - 1)], send_sem.at[1])
    wait_for(field_v.at[pl.ds(0, 8 * EDGE)], send_sem.at[2])
    wait_for(recv_d.at[pl.ds(0, NY - 1)], send_sem.at[3])
    wait_for(send_e.at[pl.ds(0, NX - 1)], send_sem.at[4])

    @pl.when(layer != 1)
    def _():
        wait_for(table_out, send_sem.at[5])


def per_device(child_out, interp, shift_angle, translators, nbr_index, nbr_trans):
    count, cols, width = child_out.shape
    children = child_out.transpose(1, 2, 0).reshape(2, RHS, width, count)
    out = pl.pallas_call(
        kernel,
        out_shape=pltpu.VMEM((cols * width, count), BF16),
        in_specs=[pl.BlockSpec(memory_space=pl.ANY)] * 6,
        out_specs=pl.BlockSpec(memory_space=pltpu.VMEM),
        scratch_shapes=[
            pltpu.VMEM((2, RHS, 32, LANES), BF16),
            pltpu.VMEM((NX, 32, WIDE), BF16),
            pltpu.VMEM((8, WIDE), F32),
            pltpu.VMEM((NT, 2, LANES), F32),
            pltpu.VMEM((NBR, 1024), jnp.int32),
            pltpu.VMEM((NBR, 1024), jnp.int32),
            pltpu.VMEM((NX, 2, 32, LANES), BF16),
            pltpu.VMEM((8, WIDE), F32),
            pltpu.VMEM((8, WIDE), F32),
            pltpu.VMEM((NT_SENT, 2 * LANES), BF16),
            pltpu.VMEM((NT_PAD, 2 * LANES), BF16),
            pltpu.VMEM((NY, 2, BLK, LANES), BF16),
            pltpu.VMEM((NY, 2, BLK, LANES), BF16),
            pltpu.VMEM((HALO_PAD, 2 * LANES), BF16),
            pltpu.VMEM((GROUP, 2 * LANES), BF16),
            pltpu.VMEM((NBR * GROUP, HALO_PAD), BF16),
            pltpu.VMEM((NBR * GROUP, 2 * LANES), F32),
            pltpu.VMEM((LAYERS, 2, BLK, LANES), BF16),
            pltpu.VMEM((NY, 2, BLK, LANES), BF16),
            pltpu.VMEM((NY, 2, BLK, LANES), F32),
            pltpu.VMEM((2 * LANES, WIDE), BF16),
            pltpu.VMEM((NX, 2, 32, LANES), BF16),
            pltpu.VMEM((NX, 2, 32, LANES), BF16),
            pltpu.SemaphoreType.DMA((12,)),
            pltpu.SemaphoreType.DMA((6,)),
            pltpu.SemaphoreType.DMA((6,)),
        ],
        compiler_params=pltpu.CompilerParams(
            collective_id=0, has_side_effects=True, vmem_limit_bytes=60 * 1024 * 1024
        ),
    )(
        children,
        interp.reshape(NX, 2, 32, NPD),
        shift_angle,
        translators,
        nbr_index.T,
        nbr_trans.T,
    )
    return out.reshape(cols, width, count).transpose(2, 0, 1)


def solution(mesh):
    return jax.shard_map(
        per_device,
        mesh=mesh,
        in_specs=(P("box", None, "dir"), P(), P(), P(None, None, "dir"), P(), P()),
        out_specs=P("box", None, "dir"),
        check_vma=False,
    )
```

```python
import jax
import jax.numpy as jnp
from jax import lax
from jax.experimental import pallas as pl
from jax.experimental.pallas import tpu as pltpu
from jax.sharding import PartitionSpec as P

MESH = pl.DeviceIdType.MESH
F32 = jnp.float32
BF16 = jnp.bfloat16

NCD = 512
NPD = 2048
NBR = 27
NT = 343
NX = 8
NY = 8
RHS = 4
LAYERS = 4
BLK = 16
LANES = 128
GROUP = LAYERS * BLK
EDGE = 48
HALO = GROUP + 8 * EDGE
HALO_PAD = 512
NT_HALF = 176
NT_SENT = 2 * NT_HALF
MINE = BLK // 2
PAIR = 2 * NY
NT_PAD = 384
STEP = 9
TURNS = [m for m in range(9) if m != 4]


def far_first(s):
    return 4 + (1 - 2 * (s % 2)) * ((s + 1) // 2)


def kernel(
    child_hbm, interp_hbm, angle_hbm, trans_hbm, nidx_hbm, ntr_hbm, out_ref,
    child_v, interp_v, angle_v, trans_v, nidx_v, ntr_v,
    send_a, recv_a, cos_v, sin_v, table_out, table_v, send_b, recv_b, field_v, turned_v,
    pick_v, factor_v, send_d, recv_d, parent_v, back_v, send_e, recv_e,
    load_sem, send_sem, recv_sem,
):
    box = lax.axis_index("box")
    me = lax.axis_index("dir")
    layer = box // 16
    zc = box % 16
    xb = zc % 2 + 2 * ((zc // 4) % 2)
    yb = (zc // 2) % 2 + 2 * (zc // 8)
    mx = me // 2
    half = me % 2
    my = half * 4 + layer
    core = zc % 2
    part = mx % 2
    lead = mx - part

    def device(x, y):
        return ((y % 4) * 16 + zc, x * 2 + y // 4)

    def neighbour(m):
        dx, dy = m % 3 - 1, m // 3 - 1
        tx, ty = (xb - dx + 4) % 4, (yb - dy + 4) % 4
        return layer * 16 + tx % 2 + 2 * (ty % 2) + 4 * (tx // 2) + 8 * (ty // 2)

    def wait_for(ref, sem):
        pltpu.make_async_copy(ref, ref, sem).wait()

    def send(src, dst, phase, to):
        return pltpu.make_async_remote_copy(
            src_ref=src, dst_ref=dst, send_sem=send_sem.at[phase], recv_sem=recv_sem.at[phase],
            device_id=to, device_id_type=MESH,
        )

    barrier = pltpu.get_barrier_semaphore()

    def greet(t, carry):
        off = far_first(t)
        for to in (device((mx + off) % NX, my), device(mx, (my + off) % NY)):
            pl.semaphore_signal(barrier, inc=1, device_id=to, device_id_type=MESH)
        return carry

    lax.fori_loop(0, NX - 1, greet, 0)
    for m in TURNS:
        pl.semaphore_signal(barrier, inc=1, device_id=(neighbour(m), me), device_id_type=MESH)

    copies = [(child_hbm, child_v), (trans_hbm, trans_v), (nidx_hbm, nidx_v), (ntr_hbm, ntr_v)]
    for c in range(8):
        column = (lead + (c + 5 if c < 4 else 16 - c)) % NX
        at = pl.ds(pl.multiple_of(column * 256, 256), 256)
        to = pl.ds(c * 256, 256)
        copies.append((angle_hbm.at[:, at], angle_v.at[:, to]))
        copies.append((interp_hbm.at[:, half, :, at], interp_v.at[:, :, to]))
    loads = [pltpu.make_async_copy(src, dst, load_sem.at[i]) for i, (src, dst) in enumerate(copies)]
    for load in loads:
        load.start()

    loads[0].wait()
    left = lax.broadcasted_iota(jnp.int32, (32, LANES), 1) < LANES // 2

    def swap_halves(first, second):
        first, second = first.astype(F32), second.astype(F32)
        return (
            jnp.where(left, first, pltpu.roll(second, LANES // 2, 1)).astype(BF16),
            jnp.where(left, pltpu.roll(first, LANES // 2, 1), second).astype(BF16),
        )

    for c in range(RHS):
        send_a[2 * c], send_a[2 * c + 1] = swap_halves(child_v[0, c], child_v[1, c])
    recv_a[mx] = send_a[mx]
    pl.semaphore_wait(barrier, (NX - 1) + (NY - 1) + len(TURNS))

    def send_child(t, carry):
        to = (mx + far_first(t)) % NX
        send(send_a.at[to], recv_a.at[mx], 0, device(to, my)).start()
        return carry

    lax.fori_loop(0, NX - 1, send_child, 0)

    loads[1].wait()
    for h in range(2):
        table_out[:, h * LANES : (h + 1) * LANES] = jnp.concatenate(
            [trans_v[:, h, :], jnp.zeros((NT_SENT - NT, LANES), F32)], axis=0
        ).astype(BF16)
    table_v[NT_SENT:NT_PAD, :] = jnp.zeros((NT_PAD - NT_SENT, 2 * LANES), BF16)
    table_in = table_v.at[pl.ds(pl.multiple_of(core * NT_HALF, 16), NT_HALF)]
    for c in range(8):
        loads[4 + 2 * c].wait()
    cos_v[...] = jnp.cos(angle_v[...])
    sin_v[...] = jnp.sin(angle_v[...])

    loads[2].wait()
    loads[3].wait()
    lane = lax.broadcasted_iota(jnp.int32, (32, LANES), 1)

    def mine(ref):
        parts = jnp.zeros((32, LANES), jnp.int32)
        for q in range(LAYERS):
            at = pl.multiple_of(q * 256 + (zc // 8) * LANES, LANES)
            cols = jnp.concatenate(
                [ref[:, pl.ds(at, LANES)], jnp.zeros((32 - NBR, LANES), jnp.int32)], axis=0
            )
            cols = pltpu.roll(cols, (q * BLK - (zc % 8) * BLK + LANES) % LANES, 1)
            parts = jnp.where(lane // BLK == q, cols, parts)
        return parts

    source = mine(nidx_v)
    sx = source % 2 + 2 * ((source // 4) % 2) + 4 * ((source // 16) % 2) + 8 * ((source // 64) % 2)
    sy = (source // 2) % 2 + 2 * ((source // 8) % 2) + 4 * ((source // 32) % 2) + 8 * ((source // 128) % 2)
    sl = source // 256
    u = (sx - 4 * xb + 20) % 16
    v = (sy - 4 * yb + 20) % 16
    bx, x, by, y = u // 4, u % 4, v // 4, v % 4
    turn = by * 3 + bx
    base = GROUP + EDGE * (turn - (turn > 4).astype(jnp.int32))
    by_y = base + 16 * (y - (by == 0).astype(jnp.int32)) + 4 * x + sl
    by_x = base + 16 * (x - (bx == 0).astype(jnp.int32)) + 4 * y + sl
    row = jnp.where(by != 1, by_y, jnp.where(bx != 1, by_x, 16 * y + 4 * x + sl))
    source_rows = row.astype(F32).T[0:GROUP, :]
    factor_rows = mine(ntr_v).astype(F32).T[0:GROUP, :]

    slot_no = lax.broadcasted_iota(jnp.int32, (GROUP, HALO_PAD), 1).astype(F32)
    for n in range(NBR):
        pick_v[n * GROUP : (n + 1) * GROUP, :] = jnp.where(
            source_rows[:, n : n + 1] == slot_no, 1.0, 0.0
        ).astype(BF16)
    field_v[HALO:HALO_PAD, :] = jnp.zeros((HALO_PAD - HALO, 2 * LANES), BF16)

    new = lax.broadcasted_iota(jnp.int32, (LANES, LANES), 0)
    old = lax.broadcasted_iota(jnp.int32, (LANES, LANES), 1)
    by_child = jnp.where((old % 8) * 16 + old // 8 == new, 1.0, 0.0).astype(BF16)
    new = lax.broadcasted_iota(jnp.int32, (2 * GROUP, GROUP), 0)
    old = lax.broadcasted_iota(jnp.int32, (2 * GROUP, GROUP), 1)
    px = old % 2 + 2 * ((old // 4) % 2)
    py = (old // 2) % 2 + 2 * (old // 32)
    pz = (old // 8) % 4
    straight = 16 * py + 4 * px + pz
    turned = GROUP + 16 * px + 4 * py + pz
    in_order = jnp.where((straight == new) | (turned == new), 1.0, 0.0).astype(BF16)

    for c in range(8):
        loads[5 + 2 * c].wait()
    wait_for(recv_a.at[pl.ds(0, NX - 1)], recv_sem.at[0])
    children = lax.dot_general(
        by_child, recv_a[...].reshape(NCD // 2, LANES), (((1,), (1,)), ((), ())),
        preferred_element_type=F32,
    ).astype(BF16)
    my_part = part * NY + my
    for turn in (0, 3, 1, 2):
        q = (layer + turn) % LAYERS
        for w in range(2):
            first = (4 * w + q) * 256
            some = interp_v[:, :, pl.ds(pl.multiple_of(first, 256), 256)]
            prod = jnp.dot(children, some.reshape(NCD // 2, 256), preferred_element_type=F32)
            for i in range(2):
                at = pl.ds(pl.multiple_of(first + i * LANES, LANES), LANES)
                total_re = jnp.zeros((MINE, LANES), F32)
                total_im = jnp.zeros((MINE, LANES), F32)
                for o in range(8):
                    re = prod[o * 16 : o * 16 + 8, i * LANES : (i + 1) * LANES]
                    im = prod[o * 16 + 8 : o * 16 + 16, i * LANES : (i + 1) * LANES]
                    cosine = cos_v[pl.ds(o, 1), at]
                    sine = sin_v[pl.ds(o, 1), at]
                    total_re = total_re + (re * cosine - im * sine)
                    total_im = total_im + (re * sine + im * cosine)
                to = i * 4 + q
                send_b[w * NY + to] = jnp.concatenate([total_re, total_im], axis=0).astype(BF16)

                @pl.when(w * NY + to != my_part)
                def _(w=w, to=to):
                    send(
                        send_b.at[w * NY + to], recv_b.at[my_part], 1, device(lead + w, to)
                    ).start()

    recv_b[my_part] = send_b[my_part]

    even = (mx + layer) % 2
    send_table = send(
        table_out.at[pl.ds(pl.multiple_of(core * NT_HALF, 16), NT_HALF)],
        table_in,
        5,
        device((mx + even * (3 - layer) + (1 - even) * (5 + layer)) % NX, my),
    )

    @pl.when(layer != 3)
    def _():
        send_table.start()

    @pl.when(layer == 3)
    def _():
        pltpu.make_async_copy(
            table_out.at[pl.ds(pl.multiple_of(core * NT_HALF, 16), NT_HALF)], table_in, recv_sem.at[5]
        ).start()

    wait_for(recv_b.at[pl.ds(0, PAIR - 1)], recv_sem.at[1])
    whole = []
    for w in range(2):
        early = recv_b[w * NY : w * NY + 4].astype(F32)
        whole.append(early + recv_b[w * NY + 4 : w * NY + 8].astype(F32))
    whole = jnp.concatenate(
        [
            jnp.concatenate([total[:, h * 8 : h * 8 + 8] for total in whole], axis=0).reshape(GROUP, LANES)
            for h in range(2)
        ],
        axis=1,
    ).astype(BF16)
    ordered = jnp.dot(in_order, whole, preferred_element_type=F32).astype(BF16)
    field_v[0:GROUP, :] = ordered[0:GROUP]
    turned_v[...] = ordered[GROUP : 2 * GROUP]

    for fx, fy in ((3, 3), (0, 3), (1, 3), (3, 1), (3, 0), (0, 1), (1, 1), (1, 0)):
        dx = (1 if fx == 3 else -1) * (1 - 2 * (xb % 2)) if fx else 0
        dy = (1 if fy == 3 else -1) * (1 - 2 * (yb % 2)) if fy else 0
        m = (dy + 1) * 3 + dx + 1
        slot = m - (m + 4) // 9
        first = pl.multiple_of(8 - 8 * (dy if fy else dx), 16)
        at = pl.multiple_of(GROUP + EDGE * slot, 16)
        send(
            (field_v if fy else turned_v).at[pl.ds(first, EDGE)],
            field_v.at[pl.ds(at, EDGE)],
            2,
            (neighbour(m), me),
        ).start()

    wait_for(table_in, recv_sem.at[5])
    swap_table = send(table_in, table_in, 6, (box + 1 - 2 * core, me))
    swap_table.start()
    swap_table.wait_recv()
    factor_no = lax.broadcasted_iota(jnp.int32, (GROUP, NT_PAD), 1).astype(F32)
    for s in range(0, NBR, STEP):
        chosen = jnp.concatenate(
            [
                jnp.where(factor_rows[:, n : n + 1] == factor_no, 1.0, 0.0).astype(BF16)
                for n in range(s, s + STEP)
            ],
            axis=0,
        )
        factor_v[s * GROUP : (s + STEP) * GROUP, :] = jnp.dot(
            chosen, table_v[...], preferred_element_type=F32
        )

    wait_for(field_v.at[pl.ds(GROUP, 8 * EDGE)], recv_sem.at[2])
    sum_re = jnp.zeros((GROUP, LANES), F32)
    sum_im = jnp.zeros((GROUP, LANES), F32)
    for s in range(0, NBR, STEP):
        picked = jnp.dot(
            pick_v[s * GROUP : (s + STEP) * GROUP, :], field_v[...], preferred_element_type=F32
        )
        for n in range(STEP):
            re = picked[n * GROUP : (n + 1) * GROUP, 0:LANES]
            im = picked[n * GROUP : (n + 1) * GROUP, LANES : 2 * LANES]
            at = (s + n) * GROUP
            t_re = factor_v[at : at + GROUP, 0:LANES]
            t_im = factor_v[at : at + GROUP, LANES : 2 * LANES]
            sum_re = sum_re + (re * t_re - im * t_im)
            sum_im = sum_im + (re * t_im + im * t_re)
    for q in range(LAYERS):
        for w in range(2):
            rows = slice(q * BLK + w * MINE, q * BLK + (w + 1) * MINE)
            send_d[2 * q + w] = jnp.concatenate([sum_re[rows], sum_im[rows]], axis=0).astype(BF16)

    def send_sum(t, carry):
        to = (my + far_first(t // 2)) % NY
        w = (part + 1 - t % 2) % 2
        send(
            send_d.at[2 * (to % 4) + w], recv_d.at[my_part], 3, device(lead + w, to)
        ).start()
        return carry

    lax.fori_loop(0, PAIR - 1, send_sum, 0)
    recv_d[my_part] = send_d[2 * layer + part]

    wait_for(recv_d.at[pl.ds(0, PAIR - 1)], recv_sem.at[3])
    parent_v[...] = recv_d[...].astype(F32)
    for c in range(8):
        for i in range(2):
            slot = (c // 4) * NY + i * 4 + c % 4
            at = slice(c * 256 + i * LANES, c * 256 + (i + 1) * LANES)
            cosine = cos_v[:, at]
            sine = sin_v[:, at]
            for p in range(0, MINE, 2):
                backs = [[], []]
                for r in range(p, p + 2):
                    re = parent_v[slot, r : r + 1, :]
                    im = parent_v[slot, MINE + r : MINE + r + 1, :]
                    backs[0].append(re * cosine + im * sine)
                    backs[1].append(im * cosine - re * sine)
                for h in range(2):
                    first = h * 64 + p * 8
                    back_v[first : first + 16, at] = jnp.concatenate(backs[h], axis=0).astype(BF16)
    prod = 0.125 * lax.dot_general(
        interp_v[...].reshape(NCD // 2, NPD), back_v[...], (((1,), (1,)), ((), ())),
        preferred_element_type=F32,
    )
    send_e[...] = prod.astype(BF16).reshape(NX, 32, LANES)

    def send_result(t, carry):
        to = (mx + far_first(t)) % NX
        send(send_e.at[to], recv_e.at[mx], 4, device(to, my)).start()
        return carry

    lax.fori_loop(0, NX - 1, send_result, 0)
    recv_e[mx] = send_e[mx]
    wait_for(recv_e.at[pl.ds(0, NX - 1)], recv_sem.at[4])
    for c in range(RHS):
        real, imag = swap_halves(recv_e[2 * c], recv_e[2 * c + 1])
        out_ref[c * 32 : (c + 1) * 32, :] = real
        out_ref[LANES + c * 32 : LANES + (c + 1) * 32, :] = imag

    wait_for(recv_a.at[pl.ds(0, NX - 1)], send_sem.at[0])
    wait_for(send_b.at[pl.ds(0, PAIR - 1)], send_sem.at[1])
    wait_for(field_v.at[pl.ds(0, 8 * EDGE)], send_sem.at[2])
    wait_for(recv_d.at[pl.ds(0, PAIR - 1)], send_sem.at[3])
    wait_for(send_e.at[pl.ds(0, NX - 1)], send_sem.at[4])

    swap_table.wait_send()

    @pl.when(layer != 3)
    def _():
        wait_for(table_in, send_sem.at[5])


def per_device(child_out, interp, shift_angle, translators, nbr_index, nbr_trans):
    count, cols, width = child_out.shape
    children = child_out.transpose(1, 2, 0).reshape(2, RHS, width, count)
    out = pl.pallas_call(
        kernel,
        out_shape=pltpu.VMEM((cols * width, count), BF16),
        in_specs=[pl.BlockSpec(memory_space=pl.ANY)] * 6,
        out_specs=pl.BlockSpec(memory_space=pltpu.VMEM),
        scratch_shapes=[
            pltpu.VMEM((2, RHS, 32, LANES), BF16),
            pltpu.VMEM((NX, 32, NPD), BF16),
            pltpu.VMEM((8, NPD), F32),
            pltpu.VMEM((NT, 2, LANES), F32),
            pltpu.VMEM((NBR, 1024), jnp.int32),
            pltpu.VMEM((NBR, 1024), jnp.int32),
            pltpu.VMEM((NX, 32, LANES), BF16),
            pltpu.VMEM((NX, 32, LANES), BF16),
            pltpu.VMEM((8, NPD), F32),
            pltpu.VMEM((8, NPD), F32),
            pltpu.VMEM((NT_SENT, 2 * LANES), BF16),
            pltpu.VMEM((NT_PAD, 2 * LANES), BF16),
            pltpu.VMEM((PAIR, 16, LANES), BF16),
            pltpu.VMEM((PAIR, 16, LANES), BF16),
            pltpu.VMEM((HALO_PAD, 2 * LANES), BF16),
            pltpu.VMEM((GROUP, 2 * LANES), BF16),
            pltpu.VMEM((NBR * GROUP, HALO_PAD), BF16),
            pltpu.VMEM((NBR * GROUP, 2 * LANES), F32),
            pltpu.VMEM((2 * LAYERS, 16, LANES), BF16),
            pltpu.VMEM((PAIR, 16, LANES), BF16),
            pltpu.VMEM((PAIR, 16, LANES), F32),
            pltpu.VMEM((LANES, NPD), BF16),
            pltpu.VMEM((NX, 32, LANES), BF16),
            pltpu.VMEM((NX, 32, LANES), BF16),
            pltpu.SemaphoreType.DMA((20,)),
            pltpu.SemaphoreType.DMA((7,)),
            pltpu.SemaphoreType.DMA((7,)),
        ],
        compiler_params=pltpu.CompilerParams(
            collective_id=0, has_side_effects=True, vmem_limit_bytes=60 * 1024 * 1024
        ),
    )(
        children,
        interp.reshape(NX, 2, 32, NPD),
        shift_angle,
        translators,
        nbr_index.T,
        nbr_trans.T,
    )
    return out.reshape(cols, width, count).transpose(2, 0, 1)


def solution(mesh):
    return jax.shard_map(
        per_device,
        mesh=mesh,
        in_specs=(P("box", None, "dir"), P(), P(), P(None, None, "dir"), P(), P()),
        out_specs=P("box", None, "dir"),
        check_vma=False,
    )
```

```python
import jax
import jax.numpy as jnp
from jax import lax
from jax.experimental import pallas as pl
from jax.experimental.pallas import tpu as pltpu
from jax.sharding import PartitionSpec as P

MESH = pl.DeviceIdType.MESH
F32 = jnp.float32
BF16 = jnp.bfloat16

NCD = 512
NPD = 2048
NBR = 27
NT = 343
NX = 8
NY = 8
RHS = 4
LAYERS = 4
BLK = 16
LANES = 128
GROUP = LAYERS * BLK
EDGE = 48
HALO = GROUP + 8 * EDGE
HALO_PAD = 512
NT_HALF = 176
NT_SENT = 2 * NT_HALF
MINE = BLK // 2
PAIR = 2 * NY
NT_PAD = 384
STEP = 9
TURNS = [m for m in range(9) if m != 4]


def far_first(s):
    return 4 + (1 - 2 * (s % 2)) * ((s + 1) // 2)


def kernel(
    child_hbm, interp_hbm, angle_hbm, trans_hbm, nidx_hbm, ntr_hbm, out_ref,
    child_v, interp_v, angle_v, trans_v, nidx_v, ntr_v,
    send_a, recv_a, cos_v, sin_v, table_out, table_v, send_b, recv_b, field_v, turned_v,
    pick_v, factor_v, send_d, recv_d, parent_v, back_v, flip_v, send_e, recv_e,
    load_sem, send_sem, recv_sem, sum_sem,
):
    box = lax.axis_index("box")
    me = lax.axis_index("dir")
    layer = box // 16
    zc = box % 16
    xb = zc % 2 + 2 * ((zc // 4) % 2)
    yb = (zc // 2) % 2 + 2 * (zc // 8)
    mx = me // 2
    half = me % 2
    my = half * 4 + layer
    core = zc % 2
    part = mx % 2
    lead = mx - part

    def device(x, y):
        return ((y % 4) * 16 + zc, x * 2 + y // 4)

    def neighbour(m):
        dx, dy = m % 3 - 1, m // 3 - 1
        tx, ty = (xb - dx + 4) % 4, (yb - dy + 4) % 4
        return layer * 16 + tx % 2 + 2 * (ty % 2) + 4 * (tx // 2) + 8 * (ty // 2)

    def wait_for(ref, sem):
        pltpu.make_async_copy(ref, ref, sem).wait()

    def send(src, dst, phase, to):
        return pltpu.make_async_remote_copy(
            src_ref=src, dst_ref=dst, send_sem=send_sem.at[phase], recv_sem=recv_sem.at[phase],
            device_id=to, device_id_type=MESH,
        )

    barrier = pltpu.get_barrier_semaphore()

    def greet(t, carry):
        off = far_first(t)
        for to in (device((mx + off) % NX, my), device(mx, (my + off) % NY)):
            pl.semaphore_signal(barrier, inc=1, device_id=to, device_id_type=MESH)
        return carry

    lax.fori_loop(0, NX - 1, greet, 0)
    for m in TURNS:
        pl.semaphore_signal(barrier, inc=1, device_id=(neighbour(m), me), device_id_type=MESH)

    copies = [(child_hbm, child_v), (trans_hbm, trans_v), (nidx_hbm, nidx_v), (ntr_hbm, ntr_v)]
    for c in range(8):
        column = (lead + (c + 5 if c < 4 else 16 - c)) % NX
        at = pl.ds(pl.multiple_of(column * 256, 256), 256)
        to = pl.ds(c * 256, 256)
        copies.append((angle_hbm.at[:, at], angle_v.at[:, to]))
        copies.append((interp_hbm.at[:, half, :, at], interp_v.at[:, :, to]))
    loads = [pltpu.make_async_copy(src, dst, load_sem.at[i]) for i, (src, dst) in enumerate(copies)]
    for load in loads:
        load.start()

    loads[0].wait()
    left = lax.broadcasted_iota(jnp.int32, (32, LANES), 1) < LANES // 2

    def swap_halves(first, second):
        first, second = first.astype(F32), second.astype(F32)
        return (
            jnp.where(left, first, pltpu.roll(second, LANES // 2, 1)).astype(BF16),
            jnp.where(left, pltpu.roll(first, LANES // 2, 1), second).astype(BF16),
        )

    for c in range(RHS):
        send_a[2 * c], send_a[2 * c + 1] = swap_halves(child_v[0, c], child_v[1, c])
    recv_a[mx] = send_a[mx]
    pl.semaphore_wait(barrier, (NX - 1) + (NY - 1) + len(TURNS))

    def send_child(t, carry):
        to = (mx + far_first(t)) % NX
        send(send_a.at[to], recv_a.at[mx], 0, device(to, my)).start()
        return carry

    lax.fori_loop(0, NX - 1, send_child, 0)

    loads[1].wait()
    for h in range(2):
        table_out[:, h * LANES : (h + 1) * LANES] = jnp.concatenate(
            [trans_v[:, h, :], jnp.zeros((NT_SENT - NT, LANES), F32)], axis=0
        ).astype(BF16)
    table_v[NT_SENT:NT_PAD, :] = jnp.zeros((NT_PAD - NT_SENT, 2 * LANES), BF16)
    table_in = table_v.at[pl.ds(pl.multiple_of(core * NT_HALF, 16), NT_HALF)]
    for c in range(8):
        loads[4 + 2 * c].wait()
    cos_v[...] = jnp.cos(angle_v[...])
    sin_v[...] = jnp.sin(angle_v[...])

    loads[2].wait()
    loads[3].wait()
    lane = lax.broadcasted_iota(jnp.int32, (32, LANES), 1)

    def mine(ref):
        parts = jnp.zeros((32, LANES), jnp.int32)
        for q in range(LAYERS):
            at = pl.multiple_of(q * 256 + (zc // 8) * LANES, LANES)
            cols = jnp.concatenate(
                [ref[:, pl.ds(at, LANES)], jnp.zeros((32 - NBR, LANES), jnp.int32)], axis=0
            )
            cols = pltpu.roll(cols, (q * BLK - (zc % 8) * BLK + LANES) % LANES, 1)
            parts = jnp.where(lane // BLK == q, cols, parts)
        return parts

    source = mine(nidx_v)
    sx = source % 2 + 2 * ((source // 4) % 2) + 4 * ((source // 16) % 2) + 8 * ((source // 64) % 2)
    sy = (source // 2) % 2 + 2 * ((source // 8) % 2) + 4 * ((source // 32) % 2) + 8 * ((source // 128) % 2)
    sl = source // 256
    u = (sx - 4 * xb + 20) % 16
    v = (sy - 4 * yb + 20) % 16
    bx, x, by, y = u // 4, u % 4, v // 4, v % 4
    turn = by * 3 + bx
    base = GROUP + EDGE * (turn - (turn > 4).astype(jnp.int32))
    by_y = base + 16 * (y - (by == 0).astype(jnp.int32)) + 4 * x + sl
    by_x = base + 16 * (x - (bx == 0).astype(jnp.int32)) + 4 * y + sl
    row = jnp.where(by != 1, by_y, jnp.where(bx != 1, by_x, 16 * y + 4 * x + sl))
    source_rows = row.astype(F32).T[0:GROUP, :]
    factor_rows = mine(ntr_v).astype(F32).T[0:GROUP, :]

    slot_no = lax.broadcasted_iota(jnp.int32, (GROUP, HALO_PAD), 1).astype(F32)
    for n in range(NBR):
        pick_v[n * GROUP : (n + 1) * GROUP, :] = jnp.where(
            source_rows[:, n : n + 1] == slot_no, 1.0, 0.0
        ).astype(BF16)
    field_v[HALO:HALO_PAD, :] = jnp.zeros((HALO_PAD - HALO, 2 * LANES), BF16)

    new = lax.broadcasted_iota(jnp.int32, (LANES, LANES), 0)
    old = lax.broadcasted_iota(jnp.int32, (LANES, LANES), 1)
    by_child = jnp.where((old % 8) * 16 + old // 8 == new, 1.0, 0.0).astype(BF16)
    new = lax.broadcasted_iota(jnp.int32, (2 * GROUP, GROUP), 0)
    old = lax.broadcasted_iota(jnp.int32, (2 * GROUP, GROUP), 1)
    px = old % 2 + 2 * ((old // 4) % 2)
    py = (old // 2) % 2 + 2 * (old // 32)
    pz = (old // 8) % 4
    straight = 16 * py + 4 * px + pz
    turned = GROUP + 16 * px + 4 * py + pz
    in_order = jnp.where((straight == new) | (turned == new), 1.0, 0.0).astype(BF16)

    for c in range(8):
        loads[5 + 2 * c].wait()
    for d in range(PAIR):
        at = slice(d * LANES, (d + 1) * LANES)
        flip_v[at, :] = interp_v[:, :, at].reshape(NCD // 2, LANES).astype(F32).T.astype(BF16)
    wait_for(recv_a.at[pl.ds(0, NX - 1)], recv_sem.at[0])
    children = lax.dot_general(
        by_child, recv_a[...].reshape(NCD // 2, LANES), (((1,), (1,)), ((), ())),
        preferred_element_type=F32,
    ).astype(BF16)
    my_part = part * NY + my
    for turn in (0, 3, 1, 2):
        q = (layer + turn) % LAYERS
        for w in range(2):
            first = (4 * w + q) * 256
            some = interp_v[:, :, pl.ds(pl.multiple_of(first, 256), 256)]
            prod = jnp.dot(children, some.reshape(NCD // 2, 256), preferred_element_type=F32)
            for i in range(2):
                at = pl.ds(pl.multiple_of(first + i * LANES, LANES), LANES)
                total_re = jnp.zeros((MINE, LANES), F32)
                total_im = jnp.zeros((MINE, LANES), F32)
                for o in range(8):
                    re = prod[o * 16 : o * 16 + 8, i * LANES : (i + 1) * LANES]
                    im = prod[o * 16 + 8 : o * 16 + 16, i * LANES : (i + 1) * LANES]
                    cosine = cos_v[pl.ds(o, 1), at]
                    sine = sin_v[pl.ds(o, 1), at]
                    total_re = total_re + (re * cosine - im * sine)
                    total_im = total_im + (re * sine + im * cosine)
                to = i * 4 + q
                send_b[w * NY + to] = jnp.concatenate([total_re, total_im], axis=0).astype(BF16)

                @pl.when(w * NY + to != my_part)
                def _(w=w, to=to):
                    send(
                        send_b.at[w * NY + to], recv_b.at[my_part], 1, device(lead + w, to)
                    ).start()

    recv_b[my_part] = send_b[my_part]

    even = (mx + layer) % 2
    send_table = send(
        table_out.at[pl.ds(pl.multiple_of(core * NT_HALF, 16), NT_HALF)],
        table_in,
        5,
        device((mx + even * (3 - layer) + (1 - even) * (5 + layer)) % NX, my),
    )

    @pl.when(layer != 3)
    def _():
        send_table.start()

    @pl.when(layer == 3)
    def _():
        pltpu.make_async_copy(
            table_out.at[pl.ds(pl.multiple_of(core * NT_HALF, 16), NT_HALF)], table_in, recv_sem.at[5]
        ).start()

    wait_for(recv_b.at[pl.ds(0, PAIR - 1)], recv_sem.at[1])
    whole = []
    for w in range(2):
        early = recv_b[w * NY : w * NY + 4].astype(F32)
        whole.append(early + recv_b[w * NY + 4 : w * NY + 8].astype(F32))
    whole = jnp.concatenate(
        [
            jnp.concatenate([total[:, h * 8 : h * 8 + 8] for total in whole], axis=0).reshape(GROUP, LANES)
            for h in range(2)
        ],
        axis=1,
    ).astype(BF16)
    ordered = jnp.dot(in_order, whole, preferred_element_type=F32).astype(BF16)
    field_v[0:GROUP, :] = ordered[0:GROUP]
    turned_v[...] = ordered[GROUP : 2 * GROUP]

    for fx, fy in ((3, 3), (0, 3), (1, 3), (3, 1), (3, 0), (0, 1), (1, 1), (1, 0)):
        dx = (1 if fx == 3 else -1) * (1 - 2 * (xb % 2)) if fx else 0
        dy = (1 if fy == 3 else -1) * (1 - 2 * (yb % 2)) if fy else 0
        m = (dy + 1) * 3 + dx + 1
        slot = m - (m + 4) // 9
        first = pl.multiple_of(8 - 8 * (dy if fy else dx), 16)
        at = pl.multiple_of(GROUP + EDGE * slot, 16)
        send(
            (field_v if fy else turned_v).at[pl.ds(first, EDGE)],
            field_v.at[pl.ds(at, EDGE)],
            2,
            (neighbour(m), me),
        ).start()

    wait_for(table_in, recv_sem.at[5])
    swap_table = send(table_in, table_in, 6, (box + 1 - 2 * core, me))
    swap_table.start()
    swap_table.wait_recv()
    factor_no = lax.broadcasted_iota(jnp.int32, (GROUP, NT_PAD), 1).astype(F32)
    for s in range(0, NBR, STEP):
        chosen = jnp.concatenate(
            [
                jnp.where(factor_rows[:, n : n + 1] == factor_no, 1.0, 0.0).astype(BF16)
                for n in range(s, s + STEP)
            ],
            axis=0,
        )
        factor_v[s * GROUP : (s + STEP) * GROUP, :] = jnp.dot(
            chosen, table_v[...], preferred_element_type=F32
        )

    wait_for(field_v.at[pl.ds(GROUP, 8 * EDGE)], recv_sem.at[2])
    sum_re = jnp.zeros((GROUP, LANES), F32)
    sum_im = jnp.zeros((GROUP, LANES), F32)
    for s in range(0, NBR, STEP):
        picked = jnp.dot(
            pick_v[s * GROUP : (s + STEP) * GROUP, :], field_v[...], preferred_element_type=F32
        )
        for n in range(STEP):
            re = picked[n * GROUP : (n + 1) * GROUP, 0:LANES]
            im = picked[n * GROUP : (n + 1) * GROUP, LANES : 2 * LANES]
            at = (s + n) * GROUP
            t_re = factor_v[at : at + GROUP, 0:LANES]
            t_im = factor_v[at : at + GROUP, LANES : 2 * LANES]
            sum_re = sum_re + (re * t_re - im * t_im)
            sum_im = sum_im + (re * t_im + im * t_re)
    for q in range(LAYERS):
        for w in range(2):
            rows = slice(q * BLK + w * MINE, q * BLK + (w + 1) * MINE)
            send_d[2 * q + w] = jnp.concatenate([sum_re[rows], sum_im[rows]], axis=0).astype(BF16)

    def slice_at(t):
        return (part + 1 - t % 2) % 2, (my + far_first(t // 2)) % NY

    def send_sum(t, carry):
        w, to = slice_at(t)
        pltpu.make_async_remote_copy(
            src_ref=send_d.at[2 * (to % 4) + w], dst_ref=recv_d.at[my_part],
            send_sem=send_sem.at[3], recv_sem=sum_sem.at[my_part],
            device_id=device(lead + w, to), device_id_type=MESH,
        ).start()
        return carry

    lax.fori_loop(0, PAIR - 1, send_sum, 0)
    recv_d[my_part] = send_d[2 * layer + part]

    for t in range(PAIR - 1, -1, -1):
        w, to = slice_at(t)
        slot = w * NY + to
        if t < PAIR - 1:
            wait_for(recv_d.at[slot], sum_sem.at[slot])
        parent_v[t] = recv_d[slot].astype(F32)
        first = (4 * w + to % 4) * 256 + to // 4 * LANES
        at = pl.ds(pl.multiple_of(first, LANES), LANES)
        cosine = cos_v[:, at]
        sine = sin_v[:, at]
        for p in range(0, MINE, 2):
            backs = [[], []]
            for r in range(p, p + 2):
                re = parent_v[t, r : r + 1, :]
                im = parent_v[t, MINE + r : MINE + r + 1, :]
                backs[0].append(re * cosine + im * sine)
                backs[1].append(im * cosine - re * sine)
            for h in range(2):
                rows = slice(h * 64 + p * 8, h * 64 + p * 8 + 16)
                back_v[rows, at] = jnp.concatenate(backs[h], axis=0).astype(BF16)
    prod = 0.125 * jnp.dot(back_v[...], flip_v[...], preferred_element_type=F32)
    send_e[...] = prod.T.astype(BF16).reshape(NX, 32, LANES)

    def send_result(t, carry):
        to = (mx + far_first(t)) % NX
        send(send_e.at[to], recv_e.at[mx], 4, device(to, my)).start()
        return carry

    lax.fori_loop(0, NX - 1, send_result, 0)
    recv_e[mx] = send_e[mx]
    wait_for(recv_e.at[pl.ds(0, NX - 1)], recv_sem.at[4])
    for c in range(RHS):
        real, imag = swap_halves(recv_e[2 * c], recv_e[2 * c + 1])
        out_ref[c * 32 : (c + 1) * 32, :] = real
        out_ref[LANES + c * 32 : LANES + (c + 1) * 32, :] = imag

    wait_for(recv_a.at[pl.ds(0, NX - 1)], send_sem.at[0])
    wait_for(send_b.at[pl.ds(0, PAIR - 1)], send_sem.at[1])
    wait_for(field_v.at[pl.ds(0, 8 * EDGE)], send_sem.at[2])
    wait_for(recv_d.at[pl.ds(0, PAIR - 1)], send_sem.at[3])
    wait_for(send_e.at[pl.ds(0, NX - 1)], send_sem.at[4])

    swap_table.wait_send()

    @pl.when(layer != 3)
    def _():
        wait_for(table_in, send_sem.at[5])


def per_device(child_out, interp, shift_angle, translators, nbr_index, nbr_trans):
    count, cols, width = child_out.shape
    children = child_out.transpose(1, 2, 0).reshape(2, RHS, width, count)
    out = pl.pallas_call(
        kernel,
        out_shape=pltpu.VMEM((cols * width, count), BF16),
        in_specs=[pl.BlockSpec(memory_space=pl.ANY)] * 6,
        out_specs=pl.BlockSpec(memory_space=pltpu.VMEM),
        scratch_shapes=[
            pltpu.VMEM((2, RHS, 32, LANES), BF16),
            pltpu.VMEM((NX, 32, NPD), BF16),
            pltpu.VMEM((8, NPD), F32),
            pltpu.VMEM((NT, 2, LANES), F32),
            pltpu.VMEM((NBR, 1024), jnp.int32),
            pltpu.VMEM((NBR, 1024), jnp.int32),
            pltpu.VMEM((NX, 32, LANES), BF16),
            pltpu.VMEM((NX, 32, LANES), BF16),
            pltpu.VMEM((8, NPD), F32),
            pltpu.VMEM((8, NPD), F32),
            pltpu.VMEM((NT_SENT, 2 * LANES), BF16),
            pltpu.VMEM((NT_PAD, 2 * LANES), BF16),
            pltpu.VMEM((PAIR, 16, LANES), BF16),
            pltpu.VMEM((PAIR, 16, LANES), BF16),
            pltpu.VMEM((HALO_PAD, 2 * LANES), BF16),
            pltpu.VMEM((GROUP, 2 * LANES), BF16),
            pltpu.VMEM((NBR * GROUP, HALO_PAD), BF16),
            pltpu.VMEM((NBR * GROUP, 2 * LANES), F32),
            pltpu.VMEM((2 * LAYERS, 16, LANES), BF16),
            pltpu.VMEM((PAIR, 16, LANES), BF16),
            pltpu.VMEM((PAIR, 16, LANES), F32),
            pltpu.VMEM((LANES, NPD), BF16),
            pltpu.VMEM((NPD, NCD // 2), BF16),
            pltpu.VMEM((NX, 32, LANES), BF16),
            pltpu.VMEM((NX, 32, LANES), BF16),
            pltpu.SemaphoreType.DMA((20,)),
            pltpu.SemaphoreType.DMA((7,)),
            pltpu.SemaphoreType.DMA((7,)),
            pltpu.SemaphoreType.DMA((PAIR,)),
        ],
        compiler_params=pltpu.CompilerParams(
            collective_id=0, has_side_effects=True, vmem_limit_bytes=60 * 1024 * 1024
        ),
    )(
        children,
        interp.reshape(NX, 2, 32, NPD),
        shift_angle,
        translators,
        nbr_index.T,
        nbr_trans.T,
    )
    return out.reshape(cols, width, count).transpose(2, 0, 1)


def solution(mesh):
    return jax.shard_map(
        per_device,
        mesh=mesh,
        in_specs=(P("box", None, "dir"), P(), P(), P(None, None, "dir"), P(), P()),
        out_specs=P("box", None, "dir"),
        check_vma=False,
    )
```

```python
import jax
import jax.numpy as jnp
from jax import lax
from jax.experimental import pallas as pl
from jax.experimental.pallas import tpu as pltpu
from jax.sharding import PartitionSpec as P

MESH = pl.DeviceIdType.MESH
F32 = jnp.float32
BF16 = jnp.bfloat16

NCD = 512
NPD = 2048
NBR = 27
NT = 343
NX = 8
NY = 8
RHS = 4
LAYERS = 4
BLK = 16
LANES = 128
GROUP = LAYERS * BLK
EDGE = 48
HALO = GROUP + 8 * EDGE
HALO_PAD = 512
NT_HALF = 176
NT_SENT = 2 * NT_HALF
MINE = BLK // 2
PAIR = 2 * NY
NT_PAD = 384
PICKS = NBR * BLK
TURNS = [m for m in range(9) if m != 4]


def far_first(s):
    return 4 + (1 - 2 * (s % 2)) * ((s + 1) // 2)


def kernel(
    child_hbm, interp_hbm, angle_hbm, trans_hbm, nidx_hbm, ntr_hbm, out_ref,
    child_v, interp_v, angle_v, trans_v, nidx_v, ntr_v,
    send_a, recv_a, cos_v, sin_v, table_out, table_v, send_b, recv_b, field_v, turned_v,
    pick_v, factor_v, send_d, recv_d, parent_v, back_v, flip_v, send_e, recv_e,
    load_sem, send_sem, recv_sem, sum_sem,
):
    box = lax.axis_index("box")
    me = lax.axis_index("dir")
    layer = box // 16
    zc = box % 16
    xb = zc % 2 + 2 * ((zc // 4) % 2)
    yb = (zc // 2) % 2 + 2 * (zc // 8)
    mx = me // 2
    half = me % 2
    my = half * 4 + layer
    core = zc % 2
    part = mx % 2
    lead = mx - part

    def device(x, y):
        return ((y % 4) * 16 + zc, x * 2 + y // 4)

    def neighbour(m):
        dx, dy = m % 3 - 1, m // 3 - 1
        tx, ty = (xb - dx + 4) % 4, (yb - dy + 4) % 4
        return layer * 16 + tx % 2 + 2 * (ty % 2) + 4 * (tx // 2) + 8 * (ty // 2)

    def wait_for(ref, sem):
        pltpu.make_async_copy(ref, ref, sem).wait()

    def send(src, dst, phase, to):
        return pltpu.make_async_remote_copy(
            src_ref=src, dst_ref=dst, send_sem=send_sem.at[phase], recv_sem=recv_sem.at[phase],
            device_id=to, device_id_type=MESH,
        )

    barrier = pltpu.get_barrier_semaphore()

    def greet(t, carry):
        off = far_first(t)
        for to in (device((mx + off) % NX, my), device(mx, (my + off) % NY)):
            pl.semaphore_signal(barrier, inc=1, device_id=to, device_id_type=MESH)
        return carry

    lax.fori_loop(0, NX - 1, greet, 0)
    for m in TURNS:
        pl.semaphore_signal(barrier, inc=1, device_id=(neighbour(m), me), device_id_type=MESH)

    copies = [(child_hbm, child_v), (trans_hbm, trans_v), (nidx_hbm, nidx_v), (ntr_hbm, ntr_v)]
    for c in range(8):
        column = (lead + (c + 5 if c < 4 else 16 - c)) % NX
        at = pl.ds(pl.multiple_of(column * 256, 256), 256)
        to = pl.ds(c * 256, 256)
        copies.append((angle_hbm.at[:, at], angle_v.at[:, to]))
        copies.append((interp_hbm.at[:, half, :, at], interp_v.at[:, :, to]))
    loads = [pltpu.make_async_copy(src, dst, load_sem.at[i]) for i, (src, dst) in enumerate(copies)]
    for load in loads:
        load.start()

    loads[0].wait()
    left = lax.broadcasted_iota(jnp.int32, (32, LANES), 1) < LANES // 2

    def swap_halves(first, second):
        first, second = first.astype(F32), second.astype(F32)
        return (
            jnp.where(left, first, pltpu.roll(second, LANES // 2, 1)).astype(BF16),
            jnp.where(left, pltpu.roll(first, LANES // 2, 1), second).astype(BF16),
        )

    for c in range(RHS):
        send_a[2 * c], send_a[2 * c + 1] = swap_halves(child_v[0, c], child_v[1, c])
    recv_a[mx] = send_a[mx]
    pl.semaphore_wait(barrier, (NX - 1) + (NY - 1) + len(TURNS))

    def send_child(t, carry):
        to = (mx + far_first(t)) % NX
        send(send_a.at[to], recv_a.at[mx], 0, device(to, my)).start()
        return carry

    lax.fori_loop(0, NX - 1, send_child, 0)

    loads[1].wait()
    for h in range(2):
        table_out[:, h * LANES : (h + 1) * LANES] = jnp.concatenate(
            [trans_v[:, h, :], jnp.zeros((NT_SENT - NT, LANES), F32)], axis=0
        ).astype(BF16)
    table_v[NT_SENT:NT_PAD, :] = jnp.zeros((NT_PAD - NT_SENT, 2 * LANES), BF16)
    table_in = table_v.at[pl.ds(pl.multiple_of(core * NT_HALF, 16), NT_HALF)]
    for c in range(8):
        loads[4 + 2 * c].wait()
    cos_v[...] = jnp.cos(angle_v[...])
    sin_v[...] = jnp.sin(angle_v[...])

    loads[2].wait()
    loads[3].wait()
    lane = lax.broadcasted_iota(jnp.int32, (32, LANES), 1)

    def mine(ref):
        parts = jnp.zeros((32, LANES), jnp.int32)
        for q in range(LAYERS):
            at = pl.multiple_of(q * 256 + (zc // 8) * LANES, LANES)
            cols = jnp.concatenate(
                [ref[:, pl.ds(at, LANES)], jnp.zeros((32 - NBR, LANES), jnp.int32)], axis=0
            )
            cols = pltpu.roll(cols, (q * BLK - (zc % 8) * BLK + LANES) % LANES, 1)
            parts = jnp.where(lane // BLK == q, cols, parts)
        return parts

    source = mine(nidx_v)
    sx = source % 2 + 2 * ((source // 4) % 2) + 4 * ((source // 16) % 2) + 8 * ((source // 64) % 2)
    sy = (source // 2) % 2 + 2 * ((source // 8) % 2) + 4 * ((source // 32) % 2) + 8 * ((source // 128) % 2)
    sl = source // 256
    u = (sx - 4 * xb + 20) % 16
    v = (sy - 4 * yb + 20) % 16
    bx, x, by, y = u // 4, u % 4, v // 4, v % 4
    turn = by * 3 + bx
    base = GROUP + EDGE * (turn - (turn > 4).astype(jnp.int32))
    by_y = base + 16 * (y - (by == 0).astype(jnp.int32)) + 4 * x + sl
    by_x = base + 16 * (x - (bx == 0).astype(jnp.int32)) + 4 * y + sl
    row = jnp.where(by != 1, by_y, jnp.where(bx != 1, by_x, 16 * y + 4 * x + sl))
    source_rows = row.astype(F32).T[0:GROUP, :]
    factor_rows = mine(ntr_v).astype(F32).T[0:GROUP, :]

    def select(rows, count, q):
        number = lax.broadcasted_iota(jnp.int32, (BLK, count), 1).astype(F32)
        mine = rows[q * BLK : (q + 1) * BLK, :]
        return jnp.concatenate(
            [jnp.where(mine[:, n : n + 1] == number, 1.0, 0.0) for n in range(NBR)], axis=0
        ).astype(BF16)

    for q in range(LAYERS):
        pick_v[q * PICKS : (q + 1) * PICKS, :] = select(source_rows, HALO_PAD, q)
    field_v[HALO:HALO_PAD, :] = jnp.zeros((HALO_PAD - HALO, 2 * LANES), BF16)

    new = lax.broadcasted_iota(jnp.int32, (LANES, LANES), 0)
    old = lax.broadcasted_iota(jnp.int32, (LANES, LANES), 1)
    by_child = jnp.where((old % 8) * 16 + old // 8 == new, 1.0, 0.0).astype(BF16)
    new = lax.broadcasted_iota(jnp.int32, (2 * GROUP, GROUP), 0)
    old = lax.broadcasted_iota(jnp.int32, (2 * GROUP, GROUP), 1)
    px = old % 2 + 2 * ((old // 4) % 2)
    py = (old // 2) % 2 + 2 * (old // 32)
    pz = (old // 8) % 4
    straight = 16 * py + 4 * px + pz
    turned = GROUP + 16 * px + 4 * py + pz
    in_order = jnp.where((straight == new) | (turned == new), 1.0, 0.0).astype(BF16)

    for c in range(8):
        loads[5 + 2 * c].wait()
    for d in range(PAIR):
        at = slice(d * LANES, (d + 1) * LANES)
        flip_v[at, :] = interp_v[:, :, at].reshape(NCD // 2, LANES).astype(F32).T.astype(BF16)
    wait_for(recv_a.at[pl.ds(0, NX - 1)], recv_sem.at[0])
    children = lax.dot_general(
        by_child, recv_a[...].reshape(NCD // 2, LANES), (((1,), (1,)), ((), ())),
        preferred_element_type=F32,
    ).astype(BF16)
    my_part = part * NY + my
    for turn in (0, 3, 1, 2):
        q = (layer + turn) % LAYERS
        for w in range(2):
            first = (4 * w + q) * 256
            some = interp_v[:, :, pl.ds(pl.multiple_of(first, 256), 256)]
            prod = jnp.dot(children, some.reshape(NCD // 2, 256), preferred_element_type=F32)
            for i in range(2):
                at = pl.ds(pl.multiple_of(first + i * LANES, LANES), LANES)
                total_re = jnp.zeros((MINE, LANES), F32)
                total_im = jnp.zeros((MINE, LANES), F32)
                for o in range(8):
                    re = prod[o * 16 : o * 16 + 8, i * LANES : (i + 1) * LANES]
                    im = prod[o * 16 + 8 : o * 16 + 16, i * LANES : (i + 1) * LANES]
                    cosine = cos_v[pl.ds(o, 1), at]
                    sine = sin_v[pl.ds(o, 1), at]
                    total_re = total_re + (re * cosine - im * sine)
                    total_im = total_im + (re * sine + im * cosine)
                to = i * 4 + q
                send_b[w * NY + to] = jnp.concatenate([total_re, total_im], axis=0).astype(BF16)

                @pl.when(w * NY + to != my_part)
                def _(w=w, to=to):
                    send(
                        send_b.at[w * NY + to], recv_b.at[my_part], 1, device(lead + w, to)
                    ).start()

    recv_b[my_part] = send_b[my_part]

    even = (mx + layer) % 2
    send_table = send(
        table_out.at[pl.ds(pl.multiple_of(core * NT_HALF, 16), NT_HALF)],
        table_in,
        5,
        device((mx + even * (3 - layer) + (1 - even) * (5 + layer)) % NX, my),
    )

    @pl.when(layer != 3)
    def _():
        send_table.start()

    @pl.when(layer == 3)
    def _():
        pltpu.make_async_copy(
            table_out.at[pl.ds(pl.multiple_of(core * NT_HALF, 16), NT_HALF)], table_in, recv_sem.at[5]
        ).start()

    wait_for(recv_b.at[pl.ds(0, PAIR - 1)], recv_sem.at[1])
    whole = []
    for w in range(2):
        early = recv_b[w * NY : w * NY + 4].astype(F32)
        whole.append(early + recv_b[w * NY + 4 : w * NY + 8].astype(F32))
    whole = jnp.concatenate(
        [
            jnp.concatenate([total[:, h * 8 : h * 8 + 8] for total in whole], axis=0).reshape(GROUP, LANES)
            for h in range(2)
        ],
        axis=1,
    ).astype(BF16)
    ordered = jnp.dot(in_order, whole, preferred_element_type=F32).astype(BF16)
    field_v[0:GROUP, :] = ordered[0:GROUP]
    turned_v[...] = ordered[GROUP : 2 * GROUP]

    for fx, fy in ((3, 3), (0, 3), (1, 3), (3, 1), (3, 0), (0, 1), (1, 1), (1, 0)):
        dx = (1 if fx == 3 else -1) * (1 - 2 * (xb % 2)) if fx else 0
        dy = (1 if fy == 3 else -1) * (1 - 2 * (yb % 2)) if fy else 0
        m = (dy + 1) * 3 + dx + 1
        slot = m - (m + 4) // 9
        first = pl.multiple_of(8 - 8 * (dy if fy else dx), 16)
        at = pl.multiple_of(GROUP + EDGE * slot, 16)
        send(
            (field_v if fy else turned_v).at[pl.ds(first, EDGE)],
            field_v.at[pl.ds(at, EDGE)],
            2,
            (neighbour(m), me),
        ).start()

    wait_for(table_in, recv_sem.at[5])
    swap_table = send(table_in, table_in, 6, (box + 1 - 2 * core, me))
    swap_table.start()
    swap_table.wait_recv()
    for q in range(LAYERS):
        factor_v[q * PICKS : (q + 1) * PICKS, :] = jnp.dot(
            select(factor_rows, NT_PAD, q), table_v[...], preferred_element_type=F32
        )

    wait_for(field_v.at[pl.ds(GROUP, 8 * EDGE)], recv_sem.at[2])
    def slice_at(t):
        return (part + 1 - t % 2) % 2, (my + far_first(t // 2)) % NY

    for turn in (0, 3, 1, 2):
        q = (layer + turn) % LAYERS
        picked = jnp.dot(
            pick_v[pl.ds(pl.multiple_of(q * PICKS, 16), PICKS), :],
            field_v[...],
            preferred_element_type=F32,
        )
        sum_re = jnp.zeros((BLK, LANES), F32)
        sum_im = jnp.zeros((BLK, LANES), F32)
        for n in range(NBR):
            re = picked[n * BLK : (n + 1) * BLK, 0:LANES]
            im = picked[n * BLK : (n + 1) * BLK, LANES : 2 * LANES]
            at = pl.ds(pl.multiple_of(q * PICKS + n * BLK, 16), BLK)
            t_re = factor_v[at, 0:LANES]
            t_im = factor_v[at, LANES : 2 * LANES]
            sum_re = sum_re + (re * t_re - im * t_im)
            sum_im = sum_im + (re * t_im + im * t_re)
        for w in range(2):
            rows = slice(w * MINE, (w + 1) * MINE)
            send_d[2 * q + w] = jnp.concatenate([sum_re[rows], sum_im[rows]], axis=0).astype(BF16)
        for i in (1, 0):
            to = (half + i) % 2 * 4 + q
            for w in range(2):

                @pl.when(w * NY + to != my_part)
                def _(w=w, to=to, q=q):
                    pltpu.make_async_remote_copy(
                        src_ref=send_d.at[2 * q + w], dst_ref=recv_d.at[my_part],
                        send_sem=send_sem.at[3], recv_sem=sum_sem.at[my_part],
                        device_id=device(lead + w, to), device_id_type=MESH,
                    ).start()

    recv_d[my_part] = send_d[2 * layer + part]

    for t in range(PAIR - 1, -1, -1):
        w, to = slice_at(t)
        slot = w * NY + to
        if t < PAIR - 1:
            wait_for(recv_d.at[slot], sum_sem.at[slot])
        parent_v[t] = recv_d[slot].astype(F32)
        first = (4 * w + to % 4) * 256 + to // 4 * LANES
        at = pl.ds(pl.multiple_of(first, LANES), LANES)
        cosine = cos_v[:, at]
        sine = sin_v[:, at]
        for p in range(0, MINE, 2):
            backs = [[], []]
            for r in range(p, p + 2):
                re = parent_v[t, r : r + 1, :]
                im = parent_v[t, MINE + r : MINE + r + 1, :]
                backs[0].append(re * cosine + im * sine)
                backs[1].append(im * cosine - re * sine)
            for h in range(2):
                rows = slice(h * 64 + p * 8, h * 64 + p * 8 + 16)
                back_v[rows, at] = jnp.concatenate(backs[h], axis=0).astype(BF16)
    prod = 0.125 * jnp.dot(back_v[...], flip_v[...], preferred_element_type=F32)
    send_e[...] = prod.T.astype(BF16).reshape(NX, 32, LANES)

    def send_result(t, carry):
        to = (mx + far_first(t)) % NX
        send(send_e.at[to], recv_e.at[mx], 4, device(to, my)).start()
        return carry

    lax.fori_loop(0, NX - 1, send_result, 0)
    recv_e[mx] = send_e[mx]
    wait_for(recv_e.at[pl.ds(0, NX - 1)], recv_sem.at[4])
    for c in range(RHS):
        real, imag = swap_halves(recv_e[2 * c], recv_e[2 * c + 1])
        out_ref[c * 32 : (c + 1) * 32, :] = real
        out_ref[LANES + c * 32 : LANES + (c + 1) * 32, :] = imag

    wait_for(recv_a.at[pl.ds(0, NX - 1)], send_sem.at[0])
    wait_for(send_b.at[pl.ds(0, PAIR - 1)], send_sem.at[1])
    wait_for(field_v.at[pl.ds(0, 8 * EDGE)], send_sem.at[2])
    wait_for(recv_d.at[pl.ds(0, PAIR - 1)], send_sem.at[3])
    wait_for(send_e.at[pl.ds(0, NX - 1)], send_sem.at[4])

    swap_table.wait_send()

    @pl.when(layer != 3)
    def _():
        wait_for(table_in, send_sem.at[5])


def per_device(child_out, interp, shift_angle, translators, nbr_index, nbr_trans):
    count, cols, width = child_out.shape
    children = child_out.transpose(1, 2, 0).reshape(2, RHS, width, count)
    out = pl.pallas_call(
        kernel,
        out_shape=pltpu.VMEM((cols * width, count), BF16),
        in_specs=[pl.BlockSpec(memory_space=pl.ANY)] * 6,
        out_specs=pl.BlockSpec(memory_space=pltpu.VMEM),
        scratch_shapes=[
            pltpu.VMEM((2, RHS, 32, LANES), BF16),
            pltpu.VMEM((NX, 32, NPD), BF16),
            pltpu.VMEM((8, NPD), F32),
            pltpu.VMEM((NT, 2, LANES), F32),
            pltpu.VMEM((NBR, 1024), jnp.int32),
            pltpu.VMEM((NBR, 1024), jnp.int32),
            pltpu.VMEM((NX, 32, LANES), BF16),
            pltpu.VMEM((NX, 32, LANES), BF16),
            pltpu.VMEM((8, NPD), F32),
            pltpu.VMEM((8, NPD), F32),
            pltpu.VMEM((NT_SENT, 2 * LANES), BF16),
            pltpu.VMEM((NT_PAD, 2 * LANES), BF16),
            pltpu.VMEM((PAIR, 16, LANES), BF16),
            pltpu.VMEM((PAIR, 16, LANES), BF16),
            pltpu.VMEM((HALO_PAD, 2 * LANES), BF16),
            pltpu.VMEM((GROUP, 2 * LANES), BF16),
            pltpu.VMEM((NBR * GROUP, HALO_PAD), BF16),
            pltpu.VMEM((NBR * GROUP, 2 * LANES), F32),
            pltpu.VMEM((2 * LAYERS, 16, LANES), BF16),
            pltpu.VMEM((PAIR, 16, LANES), BF16),
            pltpu.VMEM((PAIR, 16, LANES), F32),
            pltpu.VMEM((LANES, NPD), BF16),
            pltpu.VMEM((NPD, NCD // 2), BF16),
            pltpu.VMEM((NX, 32, LANES), BF16),
            pltpu.VMEM((NX, 32, LANES), BF16),
            pltpu.SemaphoreType.DMA((20,)),
            pltpu.SemaphoreType.DMA((7,)),
            pltpu.SemaphoreType.DMA((7,)),
            pltpu.SemaphoreType.DMA((PAIR,)),
        ],
        compiler_params=pltpu.CompilerParams(
            collective_id=0, has_side_effects=True, vmem_limit_bytes=60 * 1024 * 1024
        ),
    )(
        children,
        interp.reshape(NX, 2, 32, NPD),
        shift_angle,
        translators,
        nbr_index.T,
        nbr_trans.T,
    )
    return out.reshape(cols, width, count).transpose(2, 0, 1)


def solution(mesh):
    return jax.shard_map(
        per_device,
        mesh=mesh,
        in_specs=(P("box", None, "dir"), P(), P(), P(None, None, "dir"), P(), P()),
        out_specs=P("box", None, "dir"),
        check_vma=False,
    )
```

```python
import jax
import jax.numpy as jnp
from jax import lax
from jax.experimental import pallas as pl
from jax.experimental.pallas import tpu as pltpu
from jax.sharding import PartitionSpec as P

MESH = pl.DeviceIdType.MESH
F32 = jnp.float32
BF16 = jnp.bfloat16

NCD = 512
NPD = 2048
NBR = 27
NT = 343
NX = 8
NY = 8
RHS = 4
LAYERS = 4
BLK = 16
LANES = 128
GROUP = LAYERS * BLK
EDGE = 48
HALO = GROUP + 8 * EDGE
HALO_PAD = 512
NT_HALF = 176
NT_SENT = 2 * NT_HALF
MINE = BLK // 2
PAIR = 2 * NY
NT_PAD = 384
STEP = 9
TURNS = [m for m in range(9) if m != 4]


def far_first(s):
    return 4 + (1 - 2 * (s % 2)) * ((s + 1) // 2)


def kernel(
    child_hbm, interp_hbm, angle_hbm, trans_hbm, nidx_hbm, ntr_hbm, out_ref,
    child_v, interp_v, angle_v, trans_v, nidx_v, ntr_v,
    send_a, recv_a, cos_v, sin_v, table_out, table_v, send_b, recv_b, field_v, turned_v,
    pick_v, factor_v, send_d, recv_d, parent_v, back_v, flip_v, send_e, recv_e,
    load_sem, send_sem, recv_sem, sum_sem,
):
    box = lax.axis_index("box")
    me = lax.axis_index("dir")
    layer = box // 16
    zc = box % 16
    xb = zc % 2 + 2 * ((zc // 4) % 2)
    yb = (zc // 2) % 2 + 2 * (zc // 8)
    mx = me // 2
    half = me % 2
    my = half * 4 + layer
    core = zc % 2
    part = mx % 2
    lead = mx - part

    def device(x, y):
        return ((y % 4) * 16 + zc, x * 2 + y // 4)

    def neighbour(m):
        dx, dy = m % 3 - 1, m // 3 - 1
        tx, ty = (xb - dx + 4) % 4, (yb - dy + 4) % 4
        return layer * 16 + tx % 2 + 2 * (ty % 2) + 4 * (tx // 2) + 8 * (ty // 2)

    def wait_for(ref, sem):
        pltpu.make_async_copy(ref, ref, sem).wait()

    def send(src, dst, phase, to):
        return pltpu.make_async_remote_copy(
            src_ref=src, dst_ref=dst, send_sem=send_sem.at[phase], recv_sem=recv_sem.at[phase],
            device_id=to, device_id_type=MESH,
        )

    barrier = pltpu.get_barrier_semaphore()

    def greet(t, carry):
        off = far_first(t)
        for to in (device((mx + off) % NX, my), device(mx, (my + off) % NY)):
            pl.semaphore_signal(barrier, inc=1, device_id=to, device_id_type=MESH)
        return carry

    lax.fori_loop(0, NX - 1, greet, 0)
    for m in TURNS:
        pl.semaphore_signal(barrier, inc=1, device_id=(neighbour(m), me), device_id_type=MESH)

    copies = [(child_hbm, child_v), (trans_hbm, trans_v), (nidx_hbm, nidx_v), (ntr_hbm, ntr_v)]
    for c in range(8):
        column = (lead + (c + 5 if c < 4 else 16 - c)) % NX
        at = pl.ds(pl.multiple_of(column * 256, 256), 256)
        to = pl.ds(c * 256, 256)
        copies.append((angle_hbm.at[:, at], angle_v.at[:, to]))
        copies.append((interp_hbm.at[:, half, :, at], interp_v.at[:, :, to]))
    loads = [pltpu.make_async_copy(src, dst, load_sem.at[i]) for i, (src, dst) in enumerate(copies)]
    for load in loads:
        load.start()

    loads[0].wait()
    left = lax.broadcasted_iota(jnp.int32, (32, LANES), 1) < LANES // 2

    def swap_halves(first, second):
        first, second = first.astype(F32), second.astype(F32)
        return (
            jnp.where(left, first, pltpu.roll(second, LANES // 2, 1)).astype(BF16),
            jnp.where(left, pltpu.roll(first, LANES // 2, 1), second).astype(BF16),
        )

    for c in range(RHS):
        send_a[2 * c], send_a[2 * c + 1] = swap_halves(child_v[0, c], child_v[1, c])
    recv_a[mx] = send_a[mx]
    pl.semaphore_wait(barrier, (NX - 1) + (NY - 1) + len(TURNS))

    def send_child(t, carry):
        to = (mx + far_first(t)) % NX
        send(send_a.at[to], recv_a.at[mx], 0, device(to, my)).start()
        return carry

    lax.fori_loop(0, NX - 1, send_child, 0)

    loads[1].wait()
    for h in range(2):
        table_out[:, h * LANES : (h + 1) * LANES] = jnp.concatenate(
            [trans_v[:, h, :], jnp.zeros((NT_SENT - NT, LANES), F32)], axis=0
        ).astype(BF16)
    table_v[NT_SENT:NT_PAD, :] = jnp.zeros((NT_PAD - NT_SENT, 2 * LANES), BF16)
    table_in = table_v.at[pl.ds(pl.multiple_of(core * NT_HALF, 16), NT_HALF)]
    for c in range(8):
        loads[4 + 2 * c].wait()
    cos_v[...] = jnp.cos(angle_v[...])
    sin_v[...] = jnp.sin(angle_v[...])

    loads[2].wait()
    loads[3].wait()
    lane = lax.broadcasted_iota(jnp.int32, (32, LANES), 1)

    def mine(ref):
        parts = jnp.zeros((32, LANES), jnp.int32)
        for q in range(LAYERS):
            at = pl.multiple_of(q * 256 + (zc // 8) * LANES, LANES)
            cols = jnp.concatenate(
                [ref[:, pl.ds(at, LANES)], jnp.zeros((32 - NBR, LANES), jnp.int32)], axis=0
            )
            cols = pltpu.roll(cols, (q * BLK - (zc % 8) * BLK + LANES) % LANES, 1)
            parts = jnp.where(lane // BLK == q, cols, parts)
        return parts

    source = mine(nidx_v)
    sx = source % 2 + 2 * ((source // 4) % 2) + 4 * ((source // 16) % 2) + 8 * ((source // 64) % 2)
    sy = (source // 2) % 2 + 2 * ((source // 8) % 2) + 4 * ((source // 32) % 2) + 8 * ((source // 128) % 2)
    sl = source // 256
    u = (sx - 4 * xb + 20) % 16
    v = (sy - 4 * yb + 20) % 16
    bx, x, by, y = u // 4, u % 4, v // 4, v % 4
    turn = by * 3 + bx
    base = GROUP + EDGE * (turn - (turn > 4).astype(jnp.int32))
    by_y = base + 16 * (y - (by == 0).astype(jnp.int32)) + 4 * x + sl
    by_x = base + 16 * (x - (bx == 0).astype(jnp.int32)) + 4 * y + sl
    row = jnp.where(by != 1, by_y, jnp.where(bx != 1, by_x, 16 * y + 4 * x + sl))
    source_rows = row.astype(F32).T[0:GROUP, :]
    factor_rows = mine(ntr_v).astype(F32).T[0:GROUP, :]

    slot_no = lax.broadcasted_iota(jnp.int32, (GROUP, HALO_PAD), 1).astype(F32)
    for n in range(NBR):
        pick_v[n * GROUP : (n + 1) * GROUP, :] = jnp.where(
            source_rows[:, n : n + 1] == slot_no, 1.0, 0.0
        ).astype(BF16)
    field_v[HALO:HALO_PAD, :] = jnp.zeros((HALO_PAD - HALO, 2 * LANES), BF16)

    new = lax.broadcasted_iota(jnp.int32, (LANES, LANES), 0)
    old = lax.broadcasted_iota(jnp.int32, (LANES, LANES), 1)
    by_child = jnp.where((old % 8) * 16 + old // 8 == new, 1.0, 0.0).astype(BF16)
    new = lax.broadcasted_iota(jnp.int32, (2 * GROUP, GROUP), 0)
    old = lax.broadcasted_iota(jnp.int32, (2 * GROUP, GROUP), 1)
    px = old % 2 + 2 * ((old // 4) % 2)
    py = (old // 2) % 2 + 2 * (old // 32)
    pz = (old // 8) % 4
    straight = 16 * py + 4 * px + pz
    turned = GROUP + 16 * px + 4 * py + pz
    in_order = jnp.where((straight == new) | (turned == new), 1.0, 0.0).astype(BF16)

    for c in range(8):
        loads[5 + 2 * c].wait()
    for d in range(PAIR):
        at = slice(d * LANES, (d + 1) * LANES)
        flip_v[at, :] = interp_v[:, :, at].reshape(NCD // 2, LANES).astype(F32).T.astype(BF16)
    wait_for(recv_a.at[pl.ds(0, NX - 1)], recv_sem.at[0])
    children = lax.dot_general(
        by_child, recv_a[...].reshape(NCD // 2, LANES), (((1,), (1,)), ((), ())),
        preferred_element_type=F32,
    ).astype(BF16)
    my_part = part * NY + my
    for turn in (0, 3, 1, 2):
        q = (layer + turn) % LAYERS
        for w in range(2):
            first = (4 * w + q) * 256
            some = interp_v[:, :, pl.ds(pl.multiple_of(first, 256), 256)]
            prod = jnp.dot(children, some.reshape(NCD // 2, 256), preferred_element_type=F32)
            for i in range(2):
                at = pl.ds(pl.multiple_of(first + i * LANES, LANES), LANES)
                total_re = jnp.zeros((MINE, LANES), F32)
                total_im = jnp.zeros((MINE, LANES), F32)
                for o in range(8):
                    re = prod[o * 16 : o * 16 + 8, i * LANES : (i + 1) * LANES]
                    im = prod[o * 16 + 8 : o * 16 + 16, i * LANES : (i + 1) * LANES]
                    cosine = cos_v[pl.ds(o, 1), at]
                    sine = sin_v[pl.ds(o, 1), at]
                    total_re = total_re + (re * cosine - im * sine)
                    total_im = total_im + (re * sine + im * cosine)
                to = i * 4 + q
                send_b[w * NY + to] = jnp.concatenate([total_re, total_im], axis=0).astype(BF16)

                @pl.when(w * NY + to != my_part)
                def _(w=w, to=to):
                    send(
                        send_b.at[w * NY + to], recv_b.at[my_part], 1, device(lead + w, to)
                    ).start()

    recv_b[my_part] = send_b[my_part]

    even = (mx + layer) % 2
    send_table = send(
        table_out.at[pl.ds(pl.multiple_of(core * NT_HALF, 16), NT_HALF)],
        table_in,
        5,
        device((mx + even * (3 - layer) + (1 - even) * (5 + layer)) % NX, my),
    )

    @pl.when(layer != 3)
    def _():
        send_table.start()

    @pl.when(layer == 3)
    def _():
        pltpu.make_async_copy(
            table_out.at[pl.ds(pl.multiple_of(core * NT_HALF, 16), NT_HALF)], table_in, recv_sem.at[5]
        ).start()

    wait_for(recv_b.at[pl.ds(0, PAIR - 1)], recv_sem.at[1])
    whole = []
    for w in range(2):
        early = recv_b[w * NY : w * NY + 4].astype(F32)
        whole.append(early + recv_b[w * NY + 4 : w * NY + 8].astype(F32))
    whole = jnp.concatenate(
        [
            jnp.concatenate([total[:, h * 8 : h * 8 + 8] for total in whole], axis=0).reshape(GROUP, LANES)
            for h in range(2)
        ],
        axis=1,
    ).astype(BF16)
    ordered = jnp.dot(in_order, whole, preferred_element_type=F32).astype(BF16)
    field_v[0:GROUP, :] = ordered[0:GROUP]
    turned_v[...] = ordered[GROUP : 2 * GROUP]

    for fx, fy in ((3, 3), (0, 3), (1, 3), (3, 1), (3, 0), (0, 1), (1, 1), (1, 0)):
        dx = (1 if fx == 3 else -1) * (1 - 2 * (xb % 2)) if fx else 0
        dy = (1 if fy == 3 else -1) * (1 - 2 * (yb % 2)) if fy else 0
        m = (dy + 1) * 3 + dx + 1
        slot = m - (m + 4) // 9
        first = pl.multiple_of(8 - 8 * (dy if fy else dx), 16)
        at = pl.multiple_of(GROUP + EDGE * slot, 16)
        send(
            (field_v if fy else turned_v).at[pl.ds(first, EDGE)],
            field_v.at[pl.ds(at, EDGE)],
            2,
            (neighbour(m), me),
        ).start()

    wait_for(table_in, recv_sem.at[5])
    swap_table = send(table_in, table_in, 6, (box + 1 - 2 * core, me))
    swap_table.start()
    swap_table.wait_recv()
    factor_no = lax.broadcasted_iota(jnp.int32, (GROUP, NT_PAD), 1).astype(F32)
    for s in range(0, NBR, STEP):
        chosen = jnp.concatenate(
            [
                jnp.where(factor_rows[:, n : n + 1] == factor_no, 1.0, 0.0).astype(BF16)
                for n in range(s, s + STEP)
            ],
            axis=0,
        )
        factor_v[s * GROUP : (s + STEP) * GROUP, :] = jnp.dot(
            chosen, table_v[...], preferred_element_type=F32
        )

    wait_for(field_v.at[pl.ds(GROUP, 8 * EDGE)], recv_sem.at[2])
    sum_re = jnp.zeros((GROUP, LANES), F32)
    sum_im = jnp.zeros((GROUP, LANES), F32)
    for s in range(0, NBR, STEP):
        picked = jnp.dot(
            pick_v[s * GROUP : (s + STEP) * GROUP, :], field_v[...], preferred_element_type=F32
        )
        for n in range(STEP):
            re = picked[n * GROUP : (n + 1) * GROUP, 0:LANES]
            im = picked[n * GROUP : (n + 1) * GROUP, LANES : 2 * LANES]
            at = (s + n) * GROUP
            t_re = factor_v[at : at + GROUP, 0:LANES]
            t_im = factor_v[at : at + GROUP, LANES : 2 * LANES]
            sum_re = sum_re + (re * t_re - im * t_im)
            sum_im = sum_im + (re * t_im + im * t_re)
    for q in range(LAYERS):
        for w in range(2):
            rows = slice(q * BLK + w * MINE, q * BLK + (w + 1) * MINE)
            send_d[2 * q + w] = jnp.concatenate([sum_re[rows], sum_im[rows]], axis=0).astype(BF16)

    def slice_at(t):
        return (part + 1 - t % 2) % 2, (my + far_first(t // 2)) % NY

    def send_sum(t, carry):
        w, to = slice_at(t)
        pltpu.make_async_remote_copy(
            src_ref=send_d.at[2 * (to % 4) + w], dst_ref=recv_d.at[my_part],
            send_sem=send_sem.at[3], recv_sem=sum_sem.at[my_part],
            device_id=device(lead + w, to), device_id_type=MESH,
        ).start()
        return carry

    lax.fori_loop(0, PAIR - 1, send_sum, 0)
    recv_d[my_part] = send_d[2 * layer + part]

    prod = jnp.zeros((LANES, NCD // 2), F32)
    weights = []
    for t in range(PAIR - 1, -1, -1):
        w, to = slice_at(t)
        slot = w * NY + to
        if t < PAIR - 1:
            wait_for(recv_d.at[slot], sum_sem.at[slot])
        parent_v[t] = recv_d[slot].astype(F32)
        first = (4 * w + to % 4) * 256 + to // 4 * LANES
        at = pl.ds(pl.multiple_of(first, LANES), LANES)
        cosine = cos_v[:, at]
        sine = sin_v[:, at]
        for p in range(0, MINE, 2):
            backs = [[], []]
            for r in range(p, p + 2):
                re = parent_v[t, r : r + 1, :]
                im = parent_v[t, MINE + r : MINE + r + 1, :]
                backs[0].append(re * cosine + im * sine)
                backs[1].append(im * cosine - re * sine)
            for h in range(2):
                rows = slice(h * 64 + p * 8, h * 64 + p * 8 + 16)
                back_v[rows, t * LANES : (t + 1) * LANES] = jnp.concatenate(backs[h], axis=0).astype(BF16)
        weights.insert(0, flip_v[at, :])
        if t % 2 == 0:
            prod = prod + jnp.dot(
                back_v[:, t * LANES : (t + 2) * LANES],
                jnp.concatenate(weights, axis=0),
                preferred_element_type=F32,
            )
            weights = []
    send_e[...] = (0.125 * prod).T.astype(BF16).reshape(NX, 32, LANES)

    def send_result(t, carry):
        to = (mx + far_first(t)) % NX
        send(send_e.at[to], recv_e.at[mx], 4, device(to, my)).start()
        return carry

    lax.fori_loop(0, NX - 1, send_result, 0)
    recv_e[mx] = send_e[mx]
    wait_for(recv_e.at[pl.ds(0, NX - 1)], recv_sem.at[4])
    for c in range(RHS):
        real, imag = swap_halves(recv_e[2 * c], recv_e[2 * c + 1])
        out_ref[c * 32 : (c + 1) * 32, :] = real
        out_ref[LANES + c * 32 : LANES + (c + 1) * 32, :] = imag

    wait_for(recv_a.at[pl.ds(0, NX - 1)], send_sem.at[0])
    wait_for(send_b.at[pl.ds(0, PAIR - 1)], send_sem.at[1])
    wait_for(field_v.at[pl.ds(0, 8 * EDGE)], send_sem.at[2])
    wait_for(recv_d.at[pl.ds(0, PAIR - 1)], send_sem.at[3])
    wait_for(send_e.at[pl.ds(0, NX - 1)], send_sem.at[4])

    swap_table.wait_send()

    @pl.when(layer != 3)
    def _():
        wait_for(table_in, send_sem.at[5])


def per_device(child_out, interp, shift_angle, translators, nbr_index, nbr_trans):
    count, cols, width = child_out.shape
    children = child_out.transpose(1, 2, 0).reshape(2, RHS, width, count)
    out = pl.pallas_call(
        kernel,
        out_shape=pltpu.VMEM((cols * width, count), BF16),
        in_specs=[pl.BlockSpec(memory_space=pl.ANY)] * 6,
        out_specs=pl.BlockSpec(memory_space=pltpu.VMEM),
        scratch_shapes=[
            pltpu.VMEM((2, RHS, 32, LANES), BF16),
            pltpu.VMEM((NX, 32, NPD), BF16),
            pltpu.VMEM((8, NPD), F32),
            pltpu.VMEM((NT, 2, LANES), F32),
            pltpu.VMEM((NBR, 1024), jnp.int32),
            pltpu.VMEM((NBR, 1024), jnp.int32),
            pltpu.VMEM((NX, 32, LANES), BF16),
            pltpu.VMEM((NX, 32, LANES), BF16),
            pltpu.VMEM((8, NPD), F32),
            pltpu.VMEM((8, NPD), F32),
            pltpu.VMEM((NT_SENT, 2 * LANES), BF16),
            pltpu.VMEM((NT_PAD, 2 * LANES), BF16),
            pltpu.VMEM((PAIR, 16, LANES), BF16),
            pltpu.VMEM((PAIR, 16, LANES), BF16),
            pltpu.VMEM((HALO_PAD, 2 * LANES), BF16),
            pltpu.VMEM((GROUP, 2 * LANES), BF16),
            pltpu.VMEM((NBR * GROUP, HALO_PAD), BF16),
            pltpu.VMEM((NBR * GROUP, 2 * LANES), F32),
            pltpu.VMEM((2 * LAYERS, 16, LANES), BF16),
            pltpu.VMEM((PAIR, 16, LANES), BF16),
            pltpu.VMEM((PAIR, 16, LANES), F32),
            pltpu.VMEM((LANES, NPD), BF16),
            pltpu.VMEM((NPD, NCD // 2), BF16),
            pltpu.VMEM((NX, 32, LANES), BF16),
            pltpu.VMEM((NX, 32, LANES), BF16),
            pltpu.SemaphoreType.DMA((20,)),
            pltpu.SemaphoreType.DMA((7,)),
            pltpu.SemaphoreType.DMA((7,)),
            pltpu.SemaphoreType.DMA((PAIR,)),
        ],
        compiler_params=pltpu.CompilerParams(
            collective_id=0, has_side_effects=True, vmem_limit_bytes=60 * 1024 * 1024
        ),
    )(
        children,
        interp.reshape(NX, 2, 32, NPD),
        shift_angle,
        translators,
        nbr_index.T,
        nbr_trans.T,
    )
    return out.reshape(cols, width, count).transpose(2, 0, 1)


def solution(mesh):
    return jax.shard_map(
        per_device,
        mesh=mesh,
        in_specs=(P("box", None, "dir"), P(), P(), P(None, None, "dir"), P(), P()),
        out_specs=P("box", None, "dir"),
        check_vma=False,
    )
```

```python
import jax
import jax.numpy as jnp
from jax import lax
from jax.experimental import pallas as pl
from jax.experimental.pallas import tpu as pltpu
from jax.sharding import PartitionSpec as P

MESH = pl.DeviceIdType.MESH
F32 = jnp.float32
BF16 = jnp.bfloat16

NCD = 512
NPD = 2048
NBR = 27
NT = 343
NX = 8
NY = 8
RHS = 4
LAYERS = 4
BLK = 16
LANES = 128
GROUP = LAYERS * BLK
EDGE = 48
HALO = GROUP + 8 * EDGE
HALO_PAD = 512
NT_HALF = 176
NT_SENT = 2 * NT_HALF
MINE = BLK // 2
PAIR = 2 * NY
NT_PAD = 384
STEP = 9
TURNS = [m for m in range(9) if m != 4]


def far_first(s):
    return 4 + (1 - 2 * (s % 2)) * ((s + 1) // 2)


def kernel(
    child_hbm, interp_hbm, angle_hbm, trans_hbm, nidx_hbm, ntr_hbm, out_ref,
    child_v, interp_v, angle_v, trans_v, nidx_v, ntr_v,
    send_a, recv_a, cos_v, sin_v, table_out, table_v, send_b, recv_b, field_v, turned_v,
    pick_v, chosen_v, factor_v, send_d, recv_d, parent_v, back_v, flip_v, send_e, recv_e,
    load_sem, send_sem, recv_sem, sum_sem,
):
    box = lax.axis_index("box")
    me = lax.axis_index("dir")
    layer = box // 16
    zc = box % 16
    xb = zc % 2 + 2 * ((zc // 4) % 2)
    yb = (zc // 2) % 2 + 2 * (zc // 8)
    mx = me // 2
    half = me % 2
    my = half * 4 + layer
    core = zc % 2
    part = mx % 2
    lead = mx - part

    def device(x, y):
        return ((y % 4) * 16 + zc, x * 2 + y // 4)

    def neighbour(m):
        dx, dy = m % 3 - 1, m // 3 - 1
        tx, ty = (xb - dx + 4) % 4, (yb - dy + 4) % 4
        return layer * 16 + tx % 2 + 2 * (ty % 2) + 4 * (tx // 2) + 8 * (ty // 2)

    def wait_for(ref, sem):
        pltpu.make_async_copy(ref, ref, sem).wait()

    def send(src, dst, phase, to):
        return pltpu.make_async_remote_copy(
            src_ref=src, dst_ref=dst, send_sem=send_sem.at[phase], recv_sem=recv_sem.at[phase],
            device_id=to, device_id_type=MESH,
        )

    barrier = pltpu.get_barrier_semaphore()

    def greet(t, carry):
        off = far_first(t)
        for to in (device((mx + off) % NX, my), device(mx, (my + off) % NY)):
            pl.semaphore_signal(barrier, inc=1, device_id=to, device_id_type=MESH)
        return carry

    lax.fori_loop(0, NX - 1, greet, 0)
    for m in TURNS:
        pl.semaphore_signal(barrier, inc=1, device_id=(neighbour(m), me), device_id_type=MESH)

    copies = [(child_hbm, child_v), (trans_hbm, trans_v), (nidx_hbm, nidx_v), (ntr_hbm, ntr_v)]
    for c in range(8):
        column = (lead + (c + 5 if c < 4 else 16 - c)) % NX
        at = pl.ds(pl.multiple_of(column * 256, 256), 256)
        to = pl.ds(c * 256, 256)
        copies.append((angle_hbm.at[:, at], angle_v.at[:, to]))
        copies.append((interp_hbm.at[:, half, :, at], interp_v.at[:, :, to]))
    loads = [pltpu.make_async_copy(src, dst, load_sem.at[i]) for i, (src, dst) in enumerate(copies)]
    for load in loads:
        load.start()

    loads[0].wait()
    left = lax.broadcasted_iota(jnp.int32, (32, LANES), 1) < LANES // 2

    def swap_halves(first, second):
        first, second = first.astype(F32), second.astype(F32)
        return (
            jnp.where(left, first, pltpu.roll(second, LANES // 2, 1)).astype(BF16),
            jnp.where(left, pltpu.roll(first, LANES // 2, 1), second).astype(BF16),
        )

    for c in range(RHS):
        send_a[2 * c], send_a[2 * c + 1] = swap_halves(child_v[0, c], child_v[1, c])
    recv_a[mx] = send_a[mx]
    pl.semaphore_wait(barrier, (NX - 1) + (NY - 1) + len(TURNS))

    def send_child(t, carry):
        to = (mx + far_first(t)) % NX
        send(send_a.at[to], recv_a.at[mx], 0, device(to, my)).start()
        return carry

    lax.fori_loop(0, NX - 1, send_child, 0)

    loads[1].wait()
    for h in range(2):
        table_out[:, h * LANES : (h + 1) * LANES] = jnp.concatenate(
            [trans_v[:, h, :], jnp.zeros((NT_SENT - NT, LANES), F32)], axis=0
        ).astype(BF16)
    table_v[NT_SENT:NT_PAD, :] = jnp.zeros((NT_PAD - NT_SENT, 2 * LANES), BF16)
    table_in = table_v.at[pl.ds(pl.multiple_of(core * NT_HALF, 16), NT_HALF)]
    for c in range(8):
        loads[4 + 2 * c].wait()
    cos_v[...] = jnp.cos(angle_v[...])
    sin_v[...] = jnp.sin(angle_v[...])

    loads[2].wait()
    loads[3].wait()
    lane = lax.broadcasted_iota(jnp.int32, (32, LANES), 1)

    def mine(ref):
        parts = jnp.zeros((32, LANES), jnp.int32)
        for q in range(LAYERS):
            at = pl.multiple_of(q * 256 + (zc // 8) * LANES, LANES)
            cols = jnp.concatenate(
                [ref[:, pl.ds(at, LANES)], jnp.zeros((32 - NBR, LANES), jnp.int32)], axis=0
            )
            cols = pltpu.roll(cols, (q * BLK - (zc % 8) * BLK + LANES) % LANES, 1)
            parts = jnp.where(lane // BLK == q, cols, parts)
        return parts

    source = mine(nidx_v)
    sx = source % 2 + 2 * ((source // 4) % 2) + 4 * ((source // 16) % 2) + 8 * ((source // 64) % 2)
    sy = (source // 2) % 2 + 2 * ((source // 8) % 2) + 4 * ((source // 32) % 2) + 8 * ((source // 128) % 2)
    sl = source // 256
    u = (sx - 4 * xb + 20) % 16
    v = (sy - 4 * yb + 20) % 16
    bx, x, by, y = u // 4, u % 4, v // 4, v % 4
    turn = by * 3 + bx
    base = GROUP + EDGE * (turn - (turn > 4).astype(jnp.int32))
    by_y = base + 16 * (y - (by == 0).astype(jnp.int32)) + 4 * x + sl
    by_x = base + 16 * (x - (bx == 0).astype(jnp.int32)) + 4 * y + sl
    row = jnp.where(by != 1, by_y, jnp.where(bx != 1, by_x, 16 * y + 4 * x + sl))
    source_rows = row.astype(F32).T[0:GROUP, :]
    factor_rows = mine(ntr_v).astype(F32).T[0:GROUP, :]

    slot_no = lax.broadcasted_iota(jnp.int32, (GROUP, HALO_PAD), 1).astype(F32)
    for n in range(NBR):
        pick_v[n * GROUP : (n + 1) * GROUP, :] = jnp.where(
            source_rows[:, n : n + 1] == slot_no, 1.0, 0.0
        ).astype(BF16)
    factor_no = lax.broadcasted_iota(jnp.int32, (GROUP, NT_PAD), 1).astype(F32)
    for n in range(NBR):
        chosen_v[n * GROUP : (n + 1) * GROUP, :] = jnp.where(
            factor_rows[:, n : n + 1] == factor_no, 1.0, 0.0
        ).astype(BF16)
    field_v[HALO:HALO_PAD, :] = jnp.zeros((HALO_PAD - HALO, 2 * LANES), BF16)

    new = lax.broadcasted_iota(jnp.int32, (LANES, LANES), 0)
    old = lax.broadcasted_iota(jnp.int32, (LANES, LANES), 1)
    by_child = jnp.where((old % 8) * 16 + old // 8 == new, 1.0, 0.0).astype(BF16)
    new = lax.broadcasted_iota(jnp.int32, (2 * GROUP, GROUP), 0)
    old = lax.broadcasted_iota(jnp.int32, (2 * GROUP, GROUP), 1)
    px = old % 2 + 2 * ((old // 4) % 2)
    py = (old // 2) % 2 + 2 * (old // 32)
    pz = (old // 8) % 4
    straight = 16 * py + 4 * px + pz
    turned = GROUP + 16 * px + 4 * py + pz
    in_order = jnp.where((straight == new) | (turned == new), 1.0, 0.0).astype(BF16)

    for c in range(8):
        loads[5 + 2 * c].wait()
    for d in range(PAIR):
        at = slice(d * LANES, (d + 1) * LANES)
        flip_v[at, :] = interp_v[:, :, at].reshape(NCD // 2, LANES).astype(F32).T.astype(BF16)
    wait_for(recv_a.at[pl.ds(0, NX - 1)], recv_sem.at[0])
    children = lax.dot_general(
        by_child, recv_a[...].reshape(NCD // 2, LANES), (((1,), (1,)), ((), ())),
        preferred_element_type=F32,
    ).astype(BF16)
    my_part = part * NY + my
    for turn in (0, 3, 1, 2):
        q = (layer + turn) % LAYERS
        for w in range(2):
            first = (4 * w + q) * 256
            some = interp_v[:, :, pl.ds(pl.multiple_of(first, 256), 256)]
            prod = jnp.dot(children, some.reshape(NCD // 2, 256), preferred_element_type=F32)
            for i in range(2):
                at = pl.ds(pl.multiple_of(first + i * LANES, LANES), LANES)
                total_re = jnp.zeros((MINE, LANES), F32)
                total_im = jnp.zeros((MINE, LANES), F32)
                for o in range(8):
                    re = prod[o * 16 : o * 16 + 8, i * LANES : (i + 1) * LANES]
                    im = prod[o * 16 + 8 : o * 16 + 16, i * LANES : (i + 1) * LANES]
                    cosine = cos_v[pl.ds(o, 1), at]
                    sine = sin_v[pl.ds(o, 1), at]
                    total_re = total_re + (re * cosine - im * sine)
                    total_im = total_im + (re * sine + im * cosine)
                to = i * 4 + q
                send_b[w * NY + to] = jnp.concatenate([total_re, total_im], axis=0).astype(BF16)

                @pl.when(w * NY + to != my_part)
                def _(w=w, to=to):
                    send(
                        send_b.at[w * NY + to], recv_b.at[my_part], 1, device(lead + w, to)
                    ).start()

    recv_b[my_part] = send_b[my_part]

    even = (mx + layer) % 2
    send_table = send(
        table_out.at[pl.ds(pl.multiple_of(core * NT_HALF, 16), NT_HALF)],
        table_in,
        5,
        device((mx + even * (3 - layer) + (1 - even) * (5 + layer)) % NX, my),
    )

    @pl.when(layer != 3)
    def _():
        send_table.start()

    @pl.when(layer == 3)
    def _():
        pltpu.make_async_copy(
            table_out.at[pl.ds(pl.multiple_of(core * NT_HALF, 16), NT_HALF)], table_in, recv_sem.at[5]
        ).start()

    wait_for(recv_b.at[pl.ds(0, PAIR - 1)], recv_sem.at[1])
    whole = []
    for w in range(2):
        early = recv_b[w * NY : w * NY + 4].astype(F32)
        whole.append(early + recv_b[w * NY + 4 : w * NY + 8].astype(F32))
    whole = jnp.concatenate(
        [
            jnp.concatenate([total[:, h * 8 : h * 8 + 8] for total in whole], axis=0).reshape(GROUP, LANES)
            for h in range(2)
        ],
        axis=1,
    ).astype(BF16)
    ordered = jnp.dot(in_order, whole, preferred_element_type=F32).astype(BF16)
    field_v[0:GROUP, :] = ordered[0:GROUP]
    turned_v[...] = ordered[GROUP : 2 * GROUP]

    for fx, fy in ((3, 3), (0, 3), (1, 3), (3, 1), (3, 0), (0, 1), (1, 1), (1, 0)):
        dx = (1 if fx == 3 else -1) * (1 - 2 * (xb % 2)) if fx else 0
        dy = (1 if fy == 3 else -1) * (1 - 2 * (yb % 2)) if fy else 0
        m = (dy + 1) * 3 + dx + 1
        slot = m - (m + 4) // 9
        first = pl.multiple_of(8 - 8 * (dy if fy else dx), 16)
        at = pl.multiple_of(GROUP + EDGE * slot, 16)
        send(
            (field_v if fy else turned_v).at[pl.ds(first, EDGE)],
            field_v.at[pl.ds(at, EDGE)],
            2,
            (neighbour(m), me),
        ).start()

    wait_for(table_in, recv_sem.at[5])
    swap_table = send(table_in, table_in, 6, (box + 1 - 2 * core, me))
    swap_table.start()
    swap_table.wait_recv()
    for s in range(0, NBR, STEP):
        factor_v[s * GROUP : (s + STEP) * GROUP, :] = jnp.dot(
            chosen_v[s * GROUP : (s + STEP) * GROUP, :], table_v[...], preferred_element_type=F32
        )

    wait_for(field_v.at[pl.ds(GROUP, 8 * EDGE)], recv_sem.at[2])
    sum_re = jnp.zeros((GROUP, LANES), F32)
    sum_im = jnp.zeros((GROUP, LANES), F32)
    for s in range(0, NBR, STEP):
        picked = jnp.dot(
            pick_v[s * GROUP : (s + STEP) * GROUP, :], field_v[...], preferred_element_type=F32
        )
        for n in range(STEP):
            re = picked[n * GROUP : (n + 1) * GROUP, 0:LANES]
            im = picked[n * GROUP : (n + 1) * GROUP, LANES : 2 * LANES]
            at = (s + n) * GROUP
            t_re = factor_v[at : at + GROUP, 0:LANES]
            t_im = factor_v[at : at + GROUP, LANES : 2 * LANES]
            sum_re = sum_re + (re * t_re - im * t_im)
            sum_im = sum_im + (re * t_im + im * t_re)
    for q in range(LAYERS):
        for w in range(2):
            rows = slice(q * BLK + w * MINE, q * BLK + (w + 1) * MINE)
            send_d[2 * q + w] = jnp.concatenate([sum_re[rows], sum_im[rows]], axis=0).astype(BF16)

    def slice_at(t):
        return (part + 1 - t % 2) % 2, (my + far_first(t // 2)) % NY

    def send_sum(t, carry):
        w, to = slice_at(t)
        pltpu.make_async_remote_copy(
            src_ref=send_d.at[2 * (to % 4) + w], dst_ref=recv_d.at[my_part],
            send_sem=send_sem.at[3], recv_sem=sum_sem.at[my_part],
            device_id=device(lead + w, to), device_id_type=MESH,
        ).start()
        return carry

    lax.fori_loop(0, PAIR - 1, send_sum, 0)
    recv_d[my_part] = send_d[2 * layer + part]

    for t in range(PAIR - 1, -1, -1):
        w, to = slice_at(t)
        slot = w * NY + to
        if t < PAIR - 1:
            wait_for(recv_d.at[slot], sum_sem.at[slot])
        parent_v[t] = recv_d[slot].astype(F32)
        first = (4 * w + to % 4) * 256 + to // 4 * LANES
        at = pl.ds(pl.multiple_of(first, LANES), LANES)
        cosine = cos_v[:, at]
        sine = sin_v[:, at]
        for p in range(0, MINE, 2):
            backs = [[], []]
            for r in range(p, p + 2):
                re = parent_v[t, r : r + 1, :]
                im = parent_v[t, MINE + r : MINE + r + 1, :]
                backs[0].append(re * cosine + im * sine)
                backs[1].append(im * cosine - re * sine)
            for h in range(2):
                rows = slice(h * 64 + p * 8, h * 64 + p * 8 + 16)
                back_v[rows, at] = jnp.concatenate(backs[h], axis=0).astype(BF16)
    prod = 0.125 * jnp.dot(back_v[...], flip_v[...], preferred_element_type=F32)
    send_e[...] = prod.T.astype(BF16).reshape(NX, 32, LANES)

    def send_result(t, carry):
        to = (mx + far_first(t)) % NX
        send(send_e.at[to], recv_e.at[mx], 4, device(to, my)).start()
        return carry

    lax.fori_loop(0, NX - 1, send_result, 0)
    recv_e[mx] = send_e[mx]
    wait_for(recv_e.at[pl.ds(0, NX - 1)], recv_sem.at[4])
    for c in range(RHS):
        real, imag = swap_halves(recv_e[2 * c], recv_e[2 * c + 1])
        out_ref[c * 32 : (c + 1) * 32, :] = real
        out_ref[LANES + c * 32 : LANES + (c + 1) * 32, :] = imag

    wait_for(recv_a.at[pl.ds(0, NX - 1)], send_sem.at[0])
    wait_for(send_b.at[pl.ds(0, PAIR - 1)], send_sem.at[1])
    wait_for(field_v.at[pl.ds(0, 8 * EDGE)], send_sem.at[2])
    wait_for(recv_d.at[pl.ds(0, PAIR - 1)], send_sem.at[3])
    wait_for(send_e.at[pl.ds(0, NX - 1)], send_sem.at[4])

    swap_table.wait_send()

    @pl.when(layer != 3)
    def _():
        wait_for(table_in, send_sem.at[5])


def per_device(child_out, interp, shift_angle, translators, nbr_index, nbr_trans):
    count, cols, width = child_out.shape
    children = child_out.transpose(1, 2, 0).reshape(2, RHS, width, count)
    out = pl.pallas_call(
        kernel,
        out_shape=pltpu.VMEM((cols * width, count), BF16),
        in_specs=[pl.BlockSpec(memory_space=pl.ANY)] * 6,
        out_specs=pl.BlockSpec(memory_space=pltpu.VMEM),
        scratch_shapes=[
            pltpu.VMEM((2, RHS, 32, LANES), BF16),
            pltpu.VMEM((NX, 32, NPD), BF16),
            pltpu.VMEM((8, NPD), F32),
            pltpu.VMEM((NT, 2, LANES), F32),
            pltpu.VMEM((NBR, 1024), jnp.int32),
            pltpu.VMEM((NBR, 1024), jnp.int32),
            pltpu.VMEM((NX, 32, LANES), BF16),
            pltpu.VMEM((NX, 32, LANES), BF16),
            pltpu.VMEM((8, NPD), F32),
            pltpu.VMEM((8, NPD), F32),
            pltpu.VMEM((NT_SENT, 2 * LANES), BF16),
            pltpu.VMEM((NT_PAD, 2 * LANES), BF16),
            pltpu.VMEM((PAIR, 16, LANES), BF16),
            pltpu.VMEM((PAIR, 16, LANES), BF16),
            pltpu.VMEM((HALO_PAD, 2 * LANES), BF16),
            pltpu.VMEM((GROUP, 2 * LANES), BF16),
            pltpu.VMEM((NBR * GROUP, HALO_PAD), BF16),
            pltpu.VMEM((NBR * GROUP, NT_PAD), BF16),
            pltpu.VMEM((NBR * GROUP, 2 * LANES), F32),
            pltpu.VMEM((2 * LAYERS, 16, LANES), BF16),
            pltpu.VMEM((PAIR, 16, LANES), BF16),
            pltpu.VMEM((PAIR, 16, LANES), F32),
            pltpu.VMEM((LANES, NPD), BF16),
            pltpu.VMEM((NPD, NCD // 2), BF16),
            pltpu.VMEM((NX, 32, LANES), BF16),
            pltpu.VMEM((NX, 32, LANES), BF16),
            pltpu.SemaphoreType.DMA((20,)),
            pltpu.SemaphoreType.DMA((7,)),
            pltpu.SemaphoreType.DMA((7,)),
            pltpu.SemaphoreType.DMA((PAIR,)),
        ],
        compiler_params=pltpu.CompilerParams(
            collective_id=0, has_side_effects=True, vmem_limit_bytes=60 * 1024 * 1024
        ),
    )(
        children,
        interp.reshape(NX, 2, 32, NPD),
        shift_angle,
        translators,
        nbr_index.T,
        nbr_trans.T,
    )
    return out.reshape(cols, width, count).transpose(2, 0, 1)


def solution(mesh):
    return jax.shard_map(
        per_device,
        mesh=mesh,
        in_specs=(P("box", None, "dir"), P(), P(), P(None, None, "dir"), P(), P()),
        out_specs=P("box", None, "dir"),
        check_vma=False,
    )
```
